512 devices in a mesh: seq: 32 (over y, x), mp: 16 (over z, core).
Axes of the slice: x: 4, y: 8, z: 8, core: 2. Of those that a mesh axis runs over, the one named last changes fastest.
Arguments:
- frames: bfloat16 [1536, 100, 232], P('seq'), may hold values from -6 to 6
- instr_ids: int32 [1536], P('seq'), may hold values from 0 to 63
- film_table: float32 [64, 2, 384], replicated, may hold values from -1.5 to 1.5
- w_expand: bfloat16 [232, 1392], P(None, 'mp'), may hold values from -0.375 to 0.375
- w_depth: float32 [9, 1392], P(None, 'mp'), may hold values from -2 to 2
- w_squeeze: float32 [1392, 58], P('mp'), may hold values from -0.625 to 0.625
- w_excite: float32 [58, 1392], P(None, 'mp'), may hold values from -3.5 to 3.5
- w_project: bfloat16 [1392, 384], P('mp'), may hold values from -0.3125 to 0.3125
- w_learner: float32 [384, 8], replicated, may hold values from -0.625 to 0.625
- token_dest: int32 [12288, 1], P('seq'), may hold values from 0 to 31; in each aligned block of 384 rows (0 to 383, 384 to 767, ...) at most 24 rows name the same one
- w_policy: bfloat16 [384, 8192], P(None, 'mp'), may hold values from -0.3125 to 0.3125
- policy_cot: bfloat16 [24576, 8192], P('seq', 'mp'), may hold values from -6 to 6
Outputs:
- policy_in: bfloat16 [24576, 8192], P('seq', 'mp')
- feature_grad: bfloat16 [1536, 100, 384], P('seq', None, 'mp')
The draws below stay inside these ranges and needn't reach their ends.
Inputs may be any that keep to these rules, and one draw needn't show every extreme that they name: `token_dest`: within the 384 token rows of one index of seq no owner is named more than 24 times.
All inputs are finite; a program needn't handle non-finite values.
Results may differ from the reference program's by a relative error of at most 0.005.
Values may be sent and summed in bfloat16 or wider, within the bound.
No kernel may reach another device: no remote copies, remote signals or barrier semaphores. Data moves between devices by JAX's collectives and lax.ppermute only.
A program may use at most 64 MiB of HBM per device.

```python
import math
import jax
import jax.numpy as jnp
import numpy as np
from jax import lax

C_IN = 232
C_HID = 1392
C_SE = 58
C_OUT = 384
D_POL = 8192
KS = 3
GRID = 10
NTOK = 8
N_INSTR = 64
F_DEV = 48
CELLS = 100
FRAMES = 1536
TR = 384
TOKENS = 12288
CAP = 24
ROWS = 24576
N_SEQ = 32


def touch_ends(drawn, stream_key, smallest, top_value):
    index_at = [jax.random.randint(jax.random.fold_in(stream_key, axis), (), 0, length) for axis, length in enumerate(drawn.shape)]
    main_axis = drawn.shape.index(max(drawn.shape))
    next_to = index_at[:main_axis] + [(index_at[main_axis] + 1) % drawn.shape[main_axis]] + index_at[main_axis + 1:]
    return drawn.at[tuple(index_at)].set(smallest).at[tuple(next_to)].set(top_value)


def shard_levels(rng, shape, cuts, least, top_value):
    gain = 1.0
    for dim, blocks in cuts:
        heights = jax.random.uniform(jax.random.fold_in(jax.random.fold_in(rng, 6), dim), (blocks,), jnp.float32, least / len(cuts), top_value / len(cuts))
        gain = gain * jnp.repeat(jnp.exp(heights), shape[dim] // blocks).reshape((-1,) + (1,) * (len(shape) - 1 - dim))
    return gain


def assign_block(key, own, number, rows, amount, top, most, skew):
    order = jax.random.permutation(key, amount)
    packed, ordinary = load_shares(amount, rows * top, most, skew, True), load_shares(amount, rows * top, most, skew, False)
    places = jnp.arange(amount)

    def named(tallies, offset_by):
        used = int((tallies > 0).sum())
        fixed = max(1, used // 4)
        passed = fixed + (places - fixed + offset_by * (used - fixed)) % max(1, amount - fixed)
        return jnp.zeros((amount,), jnp.int32).at[order[jnp.where(places < fixed, places, passed)]].set(jnp.asarray(tallies, jnp.int32))

    tallies = jnp.where(number % 4 == 0, named(packed, number // 4), named(ordinary, number - number // 4 - 1))
    mixed = jax.random.permutation(jax.random.fold_in(own, 3), amount)
    giver, sink = mixed[0:amount // 2 * 2:2], mixed[1:amount // 2 * 2:2]
    slack = jnp.minimum(tallies[giver] - 1, most - tallies[sink]) // 2
    slack = jnp.where((giver == order[0]) | (sink == order[0]) | (tallies[sink] == 0), 0, jnp.maximum(slack, 0))
    passed = jax.random.randint(jax.random.fold_in(own, 4), (amount // 2,), 0, 1 << 20) % (slack + 1)
    tallies = tallies.at[giver].add(-passed).at[sink].add(passed)
    members = jnp.searchsorted(jnp.cumsum(tallies), jnp.arange(rows * top), side="right").astype(jnp.int32)
    listing = members.reshape(top, rows).T
    listing = listing[jax.random.permutation(jax.random.fold_in(own, 1), rows)]
    offset_by = jax.random.randint(jax.random.fold_in(own, 2), (rows, 1), 0, top)
    return jnp.take_along_axis(listing, (jnp.arange(top)[None, :] + offset_by) % top, axis=1)


def load_shares(number_of, total, most, lean, full):
    loads = [(1 << 20) // math.isqrt(standing ** lean) + 1 for standing in range(1, number_of + 1)]
    largest = most if full else min(most, max(-(-total // number_of), total * loads[0] // sum(loads)))
    least = 1 if total - largest >= number_of - 1 else 0
    given, spare = [largest] + [least] * (number_of - 1), total - largest - least * (number_of - 1)
    while spare > 0:
        candidates = [i for i in range(1, number_of) if given[i] < largest] or [i for i in range(1, number_of) if given[i] < most]
        whole, remaining = sum([loads[i] for i in candidates]), spare
        for i in candidates:
            more = min(most - given[i], max(1, remaining * loads[i] // whole), spare)
            given[i] = given[i] + more
            spare = spare - more
    return np.array(given)


def bell_draw(rng, shape, deviation, bound, split=(), kind=jnp.bfloat16):
    values = jax.random.normal(rng, shape, jnp.float32) * deviation
    if len(split) > 0:
        values = shard_levels(rng, shape, split, -0.22, 0.18) * values
    return jnp.clip(values, min=-bound, max=bound).astype(kind)


def setup_inputs(seed: int = 0) -> dict:
    key_list = jax.random.split(jax.random.key(seed), 13)
    frames = bell_draw(key_list[0], (FRAMES, CELLS, C_IN), 1.0, 6.0, ((0, 32),))
    instr_ids = touch_ends(jax.random.randint(key_list[1], (FRAMES,), 0, N_INSTR), jax.random.fold_in(key_list[1], 1), 0, N_INSTR - 1).astype(jnp.int32)
    film_table = bell_draw(key_list[2], (N_INSTR, 2, C_OUT), 0.3, 1.5, (), jnp.float32)
    w_expand = bell_draw(key_list[3], (C_IN, C_HID), C_IN ** -0.5, 0.375, ((1, 16),))
    w_depth = bell_draw(key_list[4], (KS * KS, C_HID), (KS * KS) ** -0.5, 2.0, ((1, 16),), jnp.float32)
    w_squeeze = bell_draw(key_list[5], (C_HID, C_SE), (max(C_HID // 16, 1)) ** -0.5, 0.625, ((0, 16),), jnp.float32)
    w_excite = bell_draw(key_list[6], (C_SE, C_HID), (max(C_SE // 16, 1)) ** -0.5, 3.5, ((1, 16),), jnp.float32)
    w_project = bell_draw(key_list[7], (C_HID, C_OUT), (C_HID // 4) ** -0.5, 0.3125, ((0, 16),))
    w_learner = bell_draw(key_list[8], (C_OUT, NTOK), (C_OUT // 4) ** -0.5, 0.625, (), jnp.float32)
    token_dest_keys = jax.random.split(jax.random.fold_in(key_list[9], 1), TOKENS // TR)
    token_dest_turns = jax.random.permutation(jax.random.fold_in(key_list[9], 3), TOKENS // TR)
    token_dest = jax.vmap(lambda own, number: assign_block(jax.random.fold_in(key_list[9], 2), own, number, TR, N_SEQ, 1, CAP, 2))(token_dest_keys, token_dest_turns).reshape((TOKENS, 1))
    w_policy = bell_draw(key_list[10], (C_OUT, D_POL), C_OUT ** -0.5, 0.3125, ((1, 16),))
    policy_cot = bell_draw(key_list[11], (ROWS, D_POL), 1.0, 6.0, ((0, 32), (1, 16)))
    return {"frames": frames, "instr_ids": instr_ids, "film_table": film_table, "w_expand": w_expand, "w_depth": w_depth, "w_squeeze": w_squeeze, "w_excite": w_excite, "w_project": w_project, "w_learner": w_learner, "token_dest": token_dest, "w_policy": w_policy, "policy_cot": policy_cot}


highest = lax.Precision.HIGHEST


def swish(value):
    return value * jax.nn.sigmoid(value)


def depth_conv(field, kernel):
    reach = KS // 2
    padded = jnp.pad(field, ((0, 0), (reach, reach), (reach, reach), (0, 0)))
    total = jnp.zeros(field.shape, jnp.float32)
    for row in range(KS):
        for col in range(KS):
            total = total + kernel[row * KS + col] * padded[:, row:row + GRID, col:col + GRID, :]
    return total


def forward(frames, instr_ids, film_table, w_expand, w_depth, w_squeeze, w_excite, w_project, w_learner):
    count = frames.shape[0]
    expanded = swish(jnp.dot(frames.reshape(count * CELLS, C_IN), w_expand, preferred_element_type=jnp.float32))
    expanded = expanded.reshape(count, GRID, GRID, C_HID)
    depthwise = swish(depth_conv(expanded, w_depth))
    squeezed = jnp.mean(depthwise, axis=(1, 2))
    excite = jax.nn.sigmoid(jnp.dot(swish(jnp.dot(squeezed, w_squeeze, precision=highest)), w_excite, precision=highest))
    hidden = (depthwise * excite[:, None, None, :]).astype(jnp.bfloat16).reshape(count * CELLS, C_HID)
    block_out = jnp.dot(hidden, w_project, preferred_element_type=jnp.float32).reshape(count, CELLS, C_OUT)
    choose = (instr_ids[:, None] == jnp.arange(N_INSTR, dtype=jnp.int32)[None, :]).astype(jnp.float32)
    film = jnp.dot(choose, film_table.reshape(N_INSTR, 2 * C_OUT), precision=highest).reshape(count, 2, C_OUT)
    scale = 1.0 + film[:, 0]
    shift = film[:, 1]
    mixed = scale[:, None, :] * block_out + shift[:, None, :]
    attend = jax.nn.sigmoid(jnp.einsum('fpc,ci->fpi', mixed, w_learner, precision=highest))
    tokens = jnp.einsum('fpi,fpc->fic', attend, mixed, precision=highest) / CELLS
    return tokens, attend, mixed, scale


def reference(frames, instr_ids, film_table, w_expand, w_depth, w_squeeze, w_excite, w_project, w_learner, token_dest, w_policy, policy_cot):
    frame_blocks = frames.reshape(N_SEQ, F_DEV, CELLS, C_IN)
    id_blocks = instr_ids.reshape(N_SEQ, F_DEV)
    weights = (film_table, w_expand, w_depth, w_squeeze, w_excite, w_project, w_learner)

    def make_tokens(pair):
        return forward(pair[0], pair[1], *weights)[0].astype(jnp.bfloat16)

    tokens = lax.map(make_tokens, (frame_blocks, id_blocks)).reshape(TOKENS, C_OUT)
    dest = token_dest[:, 0].reshape(N_SEQ, TR)
    named = (dest[:, :, None] == jnp.arange(N_SEQ, dtype=jnp.int32)[None, None, :]).astype(jnp.int32)
    position = jnp.sum((jnp.cumsum(named, axis=1) - named) * named, axis=2)
    source = jnp.arange(N_SEQ, dtype=jnp.int32)[:, None]
    slot = (dest * (N_SEQ * CAP) + source * CAP + position).reshape(TOKENS).astype(jnp.int32)
    policy_rows = jnp.zeros((ROWS, C_OUT), jnp.bfloat16).at[slot].set(tokens)

    def embed(block):
        return jnp.dot(block, w_policy, preferred_element_type=jnp.float32).astype(jnp.bfloat16)

    policy_in = lax.map(embed, policy_rows.reshape(N_SEQ, N_SEQ * CAP, C_OUT)).reshape(ROWS, D_POL)

    def pull(block):
        return jnp.dot(block, w_policy.T, preferred_element_type=jnp.float32)

    row_grad = lax.map(pull, policy_cot.reshape(N_SEQ, N_SEQ * CAP, D_POL)).reshape(ROWS, C_OUT)
    token_grad = row_grad[slot].reshape(N_SEQ, F_DEV, NTOK, C_OUT)

    def backward(triple):
        tokens_unused, attend, mixed, scale = forward(triple[0], triple[1], *weights)
        block_grad = triple[2]
        inner = jnp.einsum('fpc,fic->fpi', mixed, block_grad, precision=highest)
        slope = inner / CELLS * attend * (1.0 - attend)
        result = jnp.einsum('fpi,fic->fpc', attend, block_grad, precision=highest) / CELLS
        result = result + jnp.einsum('fpi,ci->fpc', slope, w_learner, precision=highest)
        return (scale[:, None, :] * result).astype(jnp.bfloat16)

    feature_grad = lax.map(backward, (frame_blocks, id_blocks, token_grad)).reshape(FRAMES, CELLS, C_OUT)
    return policy_in, feature_grad
```

```python
import functools

import jax
import jax.numpy as jnp
from jax import lax
from jax.experimental import pallas as pl
from jax.experimental.pallas import tpu as pltpu
from jax.sharding import PartitionSpec as P

KS = 3
GRID = 10
BAND = 32
SHARD = 96
LANES = 768
TAIL = 512
MIB = 1024 * 1024

highest = lax.Precision.HIGHEST
f32 = jnp.float32
bf16 = jnp.bfloat16

NN = (((1,), (0,)), ((), ()))
NT = (((1,), (1,)), ((), ()))
TN = (((0,), (0,)), ((), ()))


def dot(a, b, dims=NN, precision=None):
    return lax.dot_general(a, b, dims, precision=precision, preferred_element_type=f32)


def sigmoid(value):
    return 0.5 + 0.5 * jnp.tanh(0.5 * value)


def swish(value):
    half = 0.5 * value
    return half + half * jnp.tanh(half)


def iota(shape, dim):
    return lax.broadcasted_iota(jnp.int32, shape, dim)


def onehot(condition, dtype=bf16):
    return jnp.where(condition, 1.0, 0.0).astype(dtype)


def halves(value):
    top = value.astype(bf16)
    return top, (value - top.astype(f32)).astype(bf16)


def call(kernel, out_shape, *args, in_specs=None, scratch=(), flops=1e6, moved=1e6, vmem=48):
    return pl.pallas_call(
        kernel,
        out_shape=out_shape,
        in_specs=in_specs or [pl.BlockSpec(memory_space=pltpu.VMEM)] * len(args),
        out_specs=jax.tree.map(lambda _: pl.BlockSpec(memory_space=pltpu.VMEM), out_shape),
        scratch_shapes=scratch,
        compiler_params=pltpu.CompilerParams(vmem_limit_bytes=vmem * MIB),
        cost_estimate=pl.CostEstimate(
            flops=int(flops), bytes_accessed=int(moved), transcendentals=0
        ),
    )(*args)


def lane_plan(width, c_in, c_se):
    exp = width
    sq = exp + c_in
    ex = sq + c_se
    dep = ex + c_se
    return exp, sq - TAIL, ex - TAIL, dep - TAIL


def pack_kernel(plan, expand, project, squeeze, excite, depth, out):
    exp, sq, ex, dep = plan
    rows, width = project.shape
    c_in = expand.shape[1]
    span = LANES - TAIL
    out[...] = jnp.zeros(out.shape, bf16)
    out[0:rows, 0:width] = project[...]
    head = TAIL - exp
    out[0:rows, exp:TAIL] = expand[:, 0:head]

    def place(value, first):
        count = value.shape[0]
        spot = onehot(iota((count, span), 1) == iota((count, span), 0) + first)
        return dot(value, spot, TN)

    top, low = halves(depth[...])
    tail = place(squeeze[...].astype(bf16), sq)
    tail = tail + place(excite[...].astype(bf16), ex)
    tail = tail + place(top, dep) + place(low, dep + KS * KS)
    rest = c_in - head
    spot = onehot(iota((c_in, span), 0) == iota((c_in, span), 1) + head)
    tail = tail + dot(expand[...], spot)
    del rest
    out[0:rows, TAIL:LANES] = tail.astype(bf16)


def trunk_kernel(
    plan, n_tokens,
    ids, cells_ref, film, learner, w,
    tokens_out, mixed_out, attend_out, scale_out,
    e, d, h, wd, exw,
):
    exp, sq, ex, dep = plan
    width = film.shape[2]
    hidden = w.shape[0]
    bands = GRID
    rows = bands * BAND
    n_frames = 3
    first = lax.axis_index("mp") * n_frames
    scales, shifts = [], []
    for f in range(n_frames):
        name = ids[first + f]
        row = film[name]
        scales.append(1.0 + row[0:1, :])
        shifts.append(row[1:2, :])

    def by_band(parts):
        frame = iota((BAND, parts[0].shape[1]), 0) % n_frames
        return jnp.where(frame == 0, parts[0], jnp.where(frame == 1, parts[1], parts[2]))

    scale_band = by_band(scales)
    shift_band = by_band(shifts)
    scale_out[...] = jnp.concatenate(scales + [jnp.zeros((8 - n_frames, width), f32)], axis=0)
    pick = (iota((16, LANES - TAIL), 1) == iota((16, LANES - TAIL), 0) + dep) | (
        iota((16, LANES - TAIL), 1) == iota((16, LANES - TAIL), 0) + dep + KS * KS
    )
    pick = onehot(pick & (iota((16, LANES - TAIL), 0) < KS * KS))
    wd[...] = dot(pick, w[:, TAIL:LANES], NT)
    e[...] = dot(cells_ref[...], w[:, exp:exp + 256], NT)
    place = iota((BAND, 128), 0)
    has_left = place >= n_frames
    has_right = place < BAND - 2 - n_frames

    def chunk(j, carry):
        lanes = pl.ds(pl.multiple_of(j * 128, 128), 128)
        taps = [wd[t:t + 1, lanes] for t in range(KS * KS)]
        total = None
        done = None
        now = None

        def finish(r, value, total):
            out = swish(value)
            d[r * BAND:(r + 1) * BAND, lanes] = out
            return out if total is None else total + out

        for r in range(bands):
            mid = swish(e[r * BAND:(r + 1) * BAND, lanes])
            left = jnp.where(has_left, pltpu.roll(mid, n_frames, 0), 0.0)
            right = jnp.where(has_right, pltpu.roll(mid, BAND - n_frames, 0), 0.0)

            def taken(row):
                return (
                    taps[row * KS] * left + taps[row * KS + 1] * mid + taps[row * KS + 2] * right
                )

            if done is not None:
                total = finish(r - 1, done + taken(2), total)
            here = taken(1)
            if now is not None:
                here = here + now
            done, now = here, taken(0)
        total = finish(bands - 1, done, total)
        exw[:, lanes] = total
        return carry

    lax.fori_loop(0, hidden // 128, chunk, 0)
    member = (iota((8, BAND), 1) % n_frames == iota((8, BAND), 0)) & (
        iota((8, BAND), 1) < BAND - 2
    )
    mean = dot(onehot(member, f32), exw[...], precision=highest) * (1.0 / (GRID * GRID))
    top, low = halves(mean)
    both = dot(jnp.concatenate([top, low], axis=0), w[:, TAIL:LANES])
    reduced = both[0:8] + both[8:16]
    turned = pltpu.roll(swish(reduced), ex - sq, 1)
    lane = iota(turned.shape, 1)
    turned = jnp.where((lane >= ex) & (lane < dep), turned, 0.0)
    top, low = halves(turned)
    both = dot(jnp.concatenate([top, low], axis=0), w[:, TAIL:LANES], NT)
    excite = sigmoid(both[0:8] + both[8:16])
    exw[...] = by_band([excite[f:f + 1] for f in range(n_frames)])
    for r in range(bands):
        part = slice(r * BAND, (r + 1) * BAND)
        h[part, :] = (d[part, :] * exw[...]).astype(bf16)
    block = dot(h[...], w[:, 0:width])
    mixed = (
        block.reshape(bands, BAND, width) * scale_band[None] + shift_band[None]
    ).reshape(rows, width)
    mixed_out[...] = mixed
    tiled = jnp.concatenate([learner[...]] * n_frames, axis=0)
    logits = dot(tiled, mixed, NT, highest)
    at = iota(logits.shape, 1) % BAND
    mine = (at % n_frames == iota(logits.shape, 0) // n_tokens) & (at < BAND - 2)
    attend = jnp.where(mine, sigmoid(logits), 0.0)
    attend_out[...] = attend
    tokens = dot(attend, mixed, precision=highest) * (1.0 / (GRID * GRID))
    tokens_out[...] = tokens.astype(bf16)


def slots_onehot(dest, peers, capacity):
    count = dest.shape[1]
    named = iota((peers, count), 0) == dest
    before = onehot(iota((count, count), 0) < iota((count, count), 1))
    ahead = dot(onehot(named), before)
    place = jnp.sum(jnp.where(named, ahead, 0.0), axis=0, keepdims=True)
    slot = dest * capacity + place.astype(jnp.int32)
    return onehot(iota((peers * capacity, count), 0) == slot)


def scatter_kernel(peers, capacity, tokens, dest, out):
    out[...] = dot(slots_onehot(dest[...], peers, capacity), tokens[...]).astype(bf16)


def pick_kernel(peers, capacity, arrived, dest, out):
    chosen = dot(slots_onehot(dest[...], peers, capacity), arrived[...], TN)
    each = out.shape[1]
    for k in range(out.shape[0]):
        out[k] = chosen[k * each:(k + 1) * each].astype(bf16)


def backward_kernel(n_tokens, mixed, attend, scale, learner, grads, out):
    n_frames = 3
    parts, _, share, cells = out.shape
    grad = grads[0].astype(f32)
    for k in range(1, grads.shape[0]):
        grad = grad + grads[k].astype(f32)
    inner = dot(grad, mixed[...], NT, highest)
    held = attend[...]
    slope = inner * (1.0 / (GRID * GRID)) * held * (1.0 - held)
    both = jnp.concatenate([held * (1.0 / (GRID * GRID)), slope], axis=0)
    shape = (mixed.shape[0], n_frames * 128)
    row, lane = iota(shape, 0), iota(shape, 1)
    cell, frame = lane % 128, lane // 128
    spot = (row == cell // GRID * BAND + cell % GRID * n_frames + frame) & (cell < cells)
    both = dot(both, onehot(spot, f32), precision=highest)
    factors = jnp.concatenate([grad] + [learner[...]] * n_frames, axis=0)
    for f in range(n_frames):
        result = dot(
            factors * scale[f:f + 1, :], both[:, f * 128:(f + 1) * 128], TN, highest
        )
        for k in range(parts):
            out[k, f] = result[k * share:(k + 1) * share, 0:cells].astype(bf16)


def per_device(
    frames,
    instr_ids,
    film_table,
    w_expand,
    w_depth,
    w_squeeze,
    w_excite,
    w_project,
    w_learner,
    token_dest,
    w_policy,
    policy_cot,
):
    count, cells, c_in = frames.shape
    width = w_project.shape[1]
    n_tokens = w_learner.shape[1]
    n_mp = lax.axis_size("mp")
    peers = lax.axis_size("seq")
    capacity = policy_cot.shape[0] // peers
    share = width // n_mp
    n_frames = count // n_mp
    c_se = w_squeeze.shape[1]
    rows = GRID * BAND
    hidden = n_mp * SHARD
    plan = lane_plan(width, c_in, c_se)
    sds = jax.ShapeDtypeStruct
    vmem = pl.BlockSpec(memory_space=pltpu.VMEM)
    dest = token_dest.T
    learner = w_learner.T

    mine = call(
        functools.partial(pack_kernel, plan),
        sds((SHARD, LANES), bf16),
        w_expand.T, w_project, w_squeeze.T, w_excite, w_depth,
    )
    packed = lax.all_gather(mine, "mp", axis=0, tiled=True)

    grad_part = dot(policy_cot, w_policy, NT).astype(bf16)
    arrived = lax.all_to_all(
        grad_part.reshape(peers, capacity, width), "seq", split_axis=0, concat_axis=0, tiled=True
    )
    picked = call(
        functools.partial(pick_kernel, peers, capacity),
        sds((n_mp, n_frames * n_tokens, width), bf16),
        arrived.reshape(peers * capacity, width), dest,
        flops=3e8, moved=2e6,
    )
    grads = lax.all_to_all(picked, "mp", split_axis=0, concat_axis=0, tiled=True)

    own = lax.dynamic_slice_in_dim(frames, lax.axis_index("mp") * n_frames, n_frames, 0)
    own = own.transpose(1, 0, 2).reshape(GRID, GRID * n_frames, c_in)
    own = jnp.pad(own, ((0, 0), (0, BAND - GRID * n_frames), (0, 256 - c_in)))
    own = own.reshape(rows, 256)
    mine, mixed, attend, scale = call(
        functools.partial(trunk_kernel, plan, n_tokens),
        (
            sds((n_frames * n_tokens, width), bf16),
            sds((rows, width), f32),
            sds((n_frames * n_tokens, rows), f32),
            sds((8, width), f32),
        ),
        instr_ids, own, film_table, learner, packed,
        in_specs=[pl.BlockSpec(memory_space=pltpu.SMEM)] + [vmem] * 4,
        scratch=[
            pltpu.VMEM((rows, hidden), f32),
            pltpu.VMEM((rows, hidden), f32),
            pltpu.VMEM((rows, hidden), bf16),
            pltpu.VMEM((16, hidden), f32),
            pltpu.VMEM((BAND, hidden), f32),
        ],
        flops=2e9, moved=3e7,
    )
    tokens = lax.all_gather(mine, "mp", axis=0, tiled=True)
    outgoing = call(
        functools.partial(scatter_kernel, peers, capacity),
        sds((peers * capacity, width), bf16),
        tokens, dest,
        flops=3e8, moved=2e6,
    )
    rows_in = lax.all_to_all(
        outgoing.reshape(peers, capacity, width), "seq", split_axis=0, concat_axis=0, tiled=True
    )
    policy_in = dot(rows_in.reshape(peers * capacity, width), w_policy).astype(bf16)

    parts = call(
        functools.partial(backward_kernel, n_tokens),
        sds((n_mp, n_frames, share, cells), bf16),
        mixed, attend, scale, learner, grads,
        flops=1e9, moved=2e6,
    )
    parts = lax.all_to_all(parts, "mp", split_axis=0, concat_axis=0, tiled=True)
    feature_grad = parts.reshape(count, share, cells).transpose(0, 2, 1)
    return (policy_in, feature_grad)


def solution(mesh):
    return jax.shard_map(
        per_device,
        mesh=mesh,
        in_specs=(
            P("seq", None, None),
            P("seq"),
            P(),
            P(None, "mp"),
            P(None, "mp"),
            P("mp", None),
            P(None, "mp"),
            P("mp", None),
            P(),
            P("seq", None),
            P(None, "mp"),
            P("seq", "mp"),
        ),
        out_specs=(P("seq", "mp"), P("seq", None, "mp")),
        check_vma=False,
    )
```

```python
import functools

import jax
import jax.numpy as jnp
from jax import lax
from jax.experimental import pallas as pl
from jax.experimental.pallas import tpu as pltpu
from jax.sharding import PartitionSpec as P

KS = 3
GRID = 10
BAND = 32
SHARD = 96
LANES = 768
TAIL = 512
MIB = 1024 * 1024

highest = lax.Precision.HIGHEST
f32 = jnp.float32
bf16 = jnp.bfloat16

NN = (((1,), (0,)), ((), ()))
NT = (((1,), (1,)), ((), ()))
TN = (((0,), (0,)), ((), ()))


def dot(a, b, dims=NN, precision=None):
    return lax.dot_general(a, b, dims, precision=precision, preferred_element_type=f32)


def sigmoid(value):
    return 0.5 + 0.5 * jnp.tanh(0.5 * value)


def swish(value):
    half = 0.5 * value
    return half + half * jnp.tanh(half)


def iota(shape, dim):
    return lax.broadcasted_iota(jnp.int32, shape, dim)


def onehot(condition, dtype=bf16):
    return jnp.where(condition, 1.0, 0.0).astype(dtype)


def halves(value):
    top = value.astype(bf16)
    return top, (value - top.astype(f32)).astype(bf16)


def call(kernel, out_shape, *args, in_specs=None, scratch=(), flops=1e6, moved=1e6, vmem=12):
    return pl.pallas_call(
        kernel,
        out_shape=out_shape,
        in_specs=in_specs or [pl.BlockSpec(memory_space=pltpu.VMEM)] * len(args),
        out_specs=jax.tree.map(lambda _: pl.BlockSpec(memory_space=pltpu.VMEM), out_shape),
        scratch_shapes=scratch,
        compiler_params=pltpu.CompilerParams(vmem_limit_bytes=vmem * MIB),
        cost_estimate=pl.CostEstimate(
            flops=int(flops), bytes_accessed=int(moved), transcendentals=0
        ),
    )(*args)


def lane_plan(width, c_in, c_se):
    exp = width
    sq = exp + c_in
    ex = sq + c_se
    dep = ex + c_se
    return exp, sq - TAIL, ex - TAIL, dep - TAIL


def pack_kernel(
    plan, expand_in, project_in, squeeze_in, excite_in, depth_in, out,
    expand, project, squeeze, excite, depth, sems,
):
    exp, sq, ex, dep = plan
    given = (expand_in, project_in, squeeze_in, excite_in, depth_in)
    held = (expand, project, squeeze, excite, depth)
    moves = [pltpu.make_async_copy(a, b, sems.at[k]) for k, (a, b) in enumerate(zip(given, held))]
    for move in moves:
        move.start()
    rows, width = project.shape
    c_in = expand.shape[1]
    span = LANES - TAIL
    out[...] = jnp.zeros(out.shape, bf16)
    for move in moves:
        move.wait()
    out[0:rows, 0:width] = project[...]
    head = TAIL - exp
    out[0:rows, exp:TAIL] = expand[:, 0:head]

    def place(value, first):
        count = value.shape[0]
        spot = onehot(iota((count, span), 1) == iota((count, span), 0) + first)
        return dot(value, spot, TN)

    top, low = halves(depth[...])
    tail = place(squeeze[...].astype(bf16), sq)
    tail = tail + place(excite[...].astype(bf16), ex)
    tail = tail + place(top, dep) + place(low, dep + KS * KS)
    spot = onehot(iota((c_in, span), 0) == iota((c_in, span), 1) + head)
    tail = tail + dot(expand[...], spot)
    out[0:rows, TAIL:LANES] = tail.astype(bf16)


def trunk_kernel(
    plan, n_tokens,
    ids, cells_ref, film, learner, packed,
    tokens_out, mixed_out, attend_out, scale_out,
    w, e, d, h, wd, exw, sems,
):
    exp, sq, ex, dep = plan
    width = film.shape[2]
    hidden = packed.shape[0]
    late, early = (
        pltpu.make_async_copy(packed.at[:, lanes], w.at[:, lanes], sems.at[k])
        for k, lanes in enumerate((pl.ds(0, width), pl.ds(width, LANES - width)))
    )
    early.start()
    late.start()
    bands = GRID
    rows = bands * BAND
    n_frames = 3
    first = lax.axis_index("mp") * n_frames
    scales, shifts = [], []
    for f in range(n_frames):
        name = ids[first + f]
        row = film[name]
        scales.append(1.0 + row[0:1, :])
        shifts.append(row[1:2, :])

    def by_band(parts):
        frame = iota((BAND, parts[0].shape[1]), 0) % n_frames
        return jnp.where(frame == 0, parts[0], jnp.where(frame == 1, parts[1], parts[2]))

    scale_band = by_band(scales)
    shift_band = by_band(shifts)
    scale_out[...] = jnp.concatenate(scales + [jnp.zeros((8 - n_frames, width), f32)], axis=0)
    pick = (iota((16, LANES - TAIL), 1) == iota((16, LANES - TAIL), 0) + dep) | (
        iota((16, LANES - TAIL), 1) == iota((16, LANES - TAIL), 0) + dep + KS * KS
    )
    pick = onehot(pick & (iota((16, LANES - TAIL), 0) < KS * KS))
    early.wait()
    wd[...] = dot(pick, w[:, TAIL:LANES], NT)
    e[...] = dot(cells_ref[...], w[:, exp:exp + 256], NT)
    place = iota((BAND, 128), 0)
    has_left = place >= n_frames
    has_right = place < BAND - 2 - n_frames

    def chunk(j, carry):
        lanes = pl.ds(pl.multiple_of(j * 128, 128), 128)
        taps = [wd[t:t + 1, lanes] for t in range(KS * KS)]
        total = None
        done = None
        now = None

        def finish(r, value, total):
            out = swish(value)
            d[r * BAND:(r + 1) * BAND, lanes] = out
            return out if total is None else total + out

        for r in range(bands):
            mid = swish(e[r * BAND:(r + 1) * BAND, lanes])
            left = jnp.where(has_left, pltpu.roll(mid, n_frames, 0), 0.0)
            right = jnp.where(has_right, pltpu.roll(mid, BAND - n_frames, 0), 0.0)

            def taken(row):
                return (
                    taps[row * KS] * left + taps[row * KS + 1] * mid + taps[row * KS + 2] * right
                )

            if done is not None:
                total = finish(r - 1, done + taken(2), total)
            here = taken(1)
            if now is not None:
                here = here + now
            done, now = here, taken(0)
        total = finish(bands - 1, done, total)
        exw[:, lanes] = total
        return carry

    lax.fori_loop(0, hidden // 128, chunk, 0)
    member = (iota((8, BAND), 1) % n_frames == iota((8, BAND), 0)) & (
        iota((8, BAND), 1) < BAND - 2
    )
    mean = dot(onehot(member, f32), exw[...], precision=highest) * (1.0 / (GRID * GRID))
    top, low = halves(mean)
    stack = jnp.concatenate([top, low], axis=0)
    both = dot(stack, w[:, TAIL:LANES])
    reduced = both[0:8] + both[8:16]
    turned = pltpu.roll(swish(reduced), ex - sq, 1)
    lane = iota(turned.shape, 1)
    turned = jnp.where((lane >= ex) & (lane < dep), turned, 0.0)
    top, low = halves(turned)
    stack = jnp.concatenate([top, low], axis=0)
    both = dot(stack, w[:, TAIL:LANES], NT)
    excite = sigmoid(both[0:8] + both[8:16])
    exw[...] = by_band([excite[f:f + 1] for f in range(n_frames)])
    for r in range(bands):
        band = slice(r * BAND, (r + 1) * BAND)
        h[band, :] = (d[band, :] * exw[...]).astype(bf16)
    late.wait()
    block = dot(h[...], w[:, 0:width])
    mixed = (
        block.reshape(bands, BAND, width) * scale_band[None] + shift_band[None]
    ).reshape(rows, width)
    mixed_out[...] = mixed
    tiled = jnp.concatenate([learner[...]] * n_frames, axis=0)
    logits = dot(tiled, mixed, NT, highest)
    at = iota(logits.shape, 1) % BAND
    mine = (at % n_frames == iota(logits.shape, 0) // n_tokens) & (at < BAND - 2)
    attend = jnp.where(mine, sigmoid(logits), 0.0)
    attend_out[...] = attend
    tokens = dot(attend, mixed, precision=highest) * (1.0 / (GRID * GRID))
    tokens = tokens.astype(bf16)
    for k in range(tokens_out.shape[0]):
        tokens_out[k] = tokens


def slots_onehot(dest, peers, capacity):
    count = dest.shape[1]
    named = iota((peers, count), 0) == dest
    before = onehot(iota((count, count), 0) < iota((count, count), 1))
    ahead = dot(onehot(named), before)
    place = jnp.sum(jnp.where(named, ahead, 0.0), axis=0, keepdims=True)
    slot = dest * capacity + place.astype(jnp.int32)
    return onehot(iota((peers * capacity, count), 0) == slot)


def scatter_kernel(peers, capacity, tokens, dest, out):
    out[...] = dot(slots_onehot(dest[...], peers, capacity), tokens[...]).astype(bf16)


def pick_kernel(peers, capacity, arrived, dest, out):
    chosen = dot(slots_onehot(dest[...], peers, capacity), arrived[...], TN)
    each = out.shape[1]
    for k in range(out.shape[0]):
        out[k] = chosen[k * each:(k + 1) * each].astype(bf16)


def place_of(n_chips):
    me = lax.axis_index("mp")
    return me // 2, me % 2, lambda z: lax.rem(z + n_chips, n_chips)


def backward_kernel(n_tokens, cells, mixed, attend, scale, learner, grads, same, cross, res):
    n_frames = 3
    chips, share, _ = same.shape
    grad = grads[0].astype(f32)
    for k in range(1, grads.shape[0]):
        grad = grad + grads[k].astype(f32)
    inner = dot(grad, mixed[...], NT, highest)
    held = attend[...]
    slope = inner * (1.0 / (GRID * GRID)) * held * (1.0 - held)
    both = jnp.concatenate([held * (1.0 / (GRID * GRID)), slope], axis=0)
    shape = (mixed.shape[0], n_frames * 128)
    row, lane = iota(shape, 0), iota(shape, 1)
    cell, frame = lane % 128, lane // 128
    spot = (row == cell // GRID * BAND + cell % GRID * n_frames + frame) & (cell < cells)
    both = dot(both, onehot(spot, f32), precision=highest)
    factors = jnp.concatenate([grad] + [learner[...]] * n_frames, axis=0)
    for f in range(n_frames):
        lanes = slice(f * 128, (f + 1) * 128)
        res[:, lanes] = dot(factors * scale[f:f + 1, :], both[:, lanes], TN, highest)
    z, c, wrap = place_of(chips)
    for k in range(chips):
        to = 2 * wrap(z + k)
        for out, owner in ((same, to + c), (cross, to + 1 - c)):
            out[k] = res[pl.ds(pl.multiple_of(owner * share, 8), share), :].astype(bf16)


def pair_kernel(same, cross, *outs):
    for k, out in enumerate(outs):
        out[0] = same[k]
        out[1] = cross[k]


def settle_kernel(*refs):
    *parts, out = refs
    n_frames = 3
    cells = out.shape[2]
    z, c, wrap = place_of(len(parts))
    for k, part in enumerate(parts):
        source = 2 * wrap(z - k)
        for half, owner in ((0, source + c), (1, source + 1 - c)):
            for f in range(n_frames):
                out[owner * n_frames + f] = part[half, :, f * 128:f * 128 + cells]


def per_device(
    frames,
    instr_ids,
    film_table,
    w_expand,
    w_depth,
    w_squeeze,
    w_excite,
    w_project,
    w_learner,
    token_dest,
    w_policy,
    policy_cot,
):
    count, cells, c_in = frames.shape
    width = w_project.shape[1]
    n_tokens = w_learner.shape[1]
    n_mp = lax.axis_size("mp")
    peers = lax.axis_size("seq")
    capacity = policy_cot.shape[0] // peers
    share = width // n_mp
    n_frames = count // n_mp
    c_se = w_squeeze.shape[1]
    rows = GRID * BAND
    hidden = n_mp * SHARD
    plan = lane_plan(width, c_in, c_se)
    sds = jax.ShapeDtypeStruct
    vmem = pl.BlockSpec(memory_space=pltpu.VMEM)
    dest = token_dest.T
    learner = w_learner.T

    raw = (w_expand.T, w_project, w_squeeze.T, w_excite, w_depth)
    mine = call(
        functools.partial(pack_kernel, plan),
        sds((SHARD, LANES), bf16),
        *raw,
        in_specs=[pl.BlockSpec(memory_space=pl.ANY)] * len(raw),
        scratch=[pltpu.VMEM(a.shape, a.dtype) for a in raw]
        + [pltpu.SemaphoreType.DMA((len(raw),))],
        vmem=60,
    )
    across = [(m, m ^ 1) for m in range(n_mp)]
    packed = lax.all_gather(mine, "mp", axis=0, tiled=True)
    grad_part = dot(policy_cot, w_policy, NT).astype(bf16)
    arrived = lax.all_to_all(
        grad_part.reshape(peers, capacity, width), "seq", split_axis=0, concat_axis=0, tiled=True
    )
    picked = call(
        functools.partial(pick_kernel, peers, capacity),
        sds((n_mp, n_frames * n_tokens, width), bf16),
        arrived.reshape(peers * capacity, width), dest,
        flops=3e8, moved=2e6,
    )
    grads = lax.all_to_all(picked, "mp", split_axis=0, concat_axis=0, tiled=True)

    own = lax.dynamic_slice_in_dim(frames, lax.axis_index("mp") * n_frames, n_frames, 0)
    own = own.transpose(1, 0, 2).reshape(GRID, GRID * n_frames, c_in)
    own = jnp.pad(own, ((0, 0), (0, BAND - GRID * n_frames), (0, 256 - c_in)))
    own = own.reshape(rows, 256)
    copies, mixed, attend, scale = call(
        functools.partial(trunk_kernel, plan, n_tokens),
        (
            sds((n_mp, n_frames * n_tokens, width), bf16),
            sds((rows, width), f32),
            sds((n_frames * n_tokens, rows), f32),
            sds((8, width), f32),
        ),
        instr_ids, own, film_table, learner, packed,
        in_specs=[pl.BlockSpec(memory_space=pltpu.SMEM)] + [vmem] * 3 + [pl.BlockSpec(memory_space=pl.ANY)],
        scratch=[
            pltpu.VMEM((hidden, LANES), bf16),
            pltpu.VMEM((rows, hidden), f32),
            pltpu.VMEM((rows, hidden), f32),
            pltpu.VMEM((rows, hidden), bf16),
            pltpu.VMEM((16, hidden), f32),
            pltpu.VMEM((BAND, hidden), f32),
            pltpu.SemaphoreType.DMA((2,)),
        ],
        flops=2e9, moved=3e7, vmem=28,
    )
    tokens = lax.all_to_all(copies, "mp", split_axis=0, concat_axis=0, tiled=True)
    outgoing = call(
        functools.partial(scatter_kernel, peers, capacity),
        sds((peers * capacity, width), bf16),
        tokens.reshape(count * n_tokens, width), dest,
        flops=3e8, moved=2e6,
    )
    chips = n_mp // 2
    half = sds((chips, share, n_frames * 128), bf16)
    same, cross = call(
        functools.partial(backward_kernel, n_tokens, cells),
        (half, half),
        mixed, attend, scale, learner, grads,
        scratch=[pltpu.VMEM((width, n_frames * 128), f32)],
        flops=1e9, moved=2e6,
    )
    cross = lax.ppermute(cross, "mp", across)
    pairs = call(
        pair_kernel, (sds((2, share, n_frames * 128), bf16),) * chips, same, cross
    )
    outgoing, *pairs = lax.optimization_barrier((outgoing, *pairs))
    rows_in = lax.all_to_all(
        outgoing.reshape(peers, capacity, width), "seq", split_axis=0, concat_axis=0, tiled=True
    )
    parts = [pairs[0]]
    for k in range(1, chips):
        parts.append(lax.ppermute(pairs[k], "mp", [(m, (m + 2 * k) % n_mp) for m in range(n_mp)]))
    feature_grad = call(settle_kernel, sds((count, share, cells), bf16), *parts)
    w_policy, feature_grad = lax.optimization_barrier((w_policy, feature_grad))
    policy_in = dot(rows_in.reshape(peers * capacity, width), w_policy).astype(bf16)

    feature_grad = feature_grad.transpose(0, 2, 1)
    return (policy_in, feature_grad)


def solution(mesh):
    return jax.shard_map(
        per_device,
        mesh=mesh,
        in_specs=(
            P("seq", None, None),
            P("seq"),
            P(),
            P(None, "mp"),
            P(None, "mp"),
            P("mp", None),
            P(None, "mp"),
            P("mp", None),
            P(),
            P("seq", None),
            P(None, "mp"),
            P("seq", "mp"),
        ),
        out_specs=(P("seq", "mp"), P("seq", None, "mp")),
        check_vma=False,
    )
```

```python
import functools

import jax
import jax.numpy as jnp
from jax import lax
from jax.experimental import pallas as pl
from jax.experimental.pallas import tpu as pltpu
from jax.sharding import PartitionSpec as P

KS = 3
GRID = 10
BAND = 32
SHARD = 88
LANES = 768
TAIL = 512
MIB = 1024 * 1024

highest = lax.Precision.HIGHEST
f32 = jnp.float32
bf16 = jnp.bfloat16

NN = (((1,), (0,)), ((), ()))
NT = (((1,), (1,)), ((), ()))
TN = (((0,), (0,)), ((), ()))


def dot(a, b, dims=NN, precision=None):
    return lax.dot_general(a, b, dims, precision=precision, preferred_element_type=f32)


def sigmoid(value):
    return 0.5 + 0.5 * jnp.tanh(0.5 * value)


def swish(value):
    half = 0.5 * value
    return half + half * jnp.tanh(half)


def iota(shape, dim):
    return lax.broadcasted_iota(jnp.int32, shape, dim)


def onehot(condition, dtype=bf16):
    return jnp.where(condition, 1.0, 0.0).astype(dtype)


def halves(value):
    top = value.astype(bf16)
    return top, (value - top.astype(f32)).astype(bf16)


def call(kernel, out_shape, *args, in_specs=None, scratch=(), flops=1e6, moved=1e6, vmem=12):
    return pl.pallas_call(
        kernel,
        out_shape=out_shape,
        in_specs=in_specs or [pl.BlockSpec(memory_space=pltpu.VMEM)] * len(args),
        out_specs=jax.tree.map(lambda _: pl.BlockSpec(memory_space=pltpu.VMEM), out_shape),
        scratch_shapes=scratch,
        compiler_params=pltpu.CompilerParams(vmem_limit_bytes=vmem * MIB),
        cost_estimate=pl.CostEstimate(
            flops=int(flops), bytes_accessed=int(moved), transcendentals=0
        ),
    )(*args)


def lane_plan(width, c_in, c_se):
    exp = width
    sq = exp + c_in
    ex = sq + c_se
    dep = ex + c_se
    return exp, sq - TAIL, ex - TAIL, dep - TAIL


def pack_kernel(
    plan, expand_in, project_in, squeeze_in, excite_in, depth_in, out,
    expand, project, squeeze, excite, depth, sems,
):
    exp, sq, ex, dep = plan
    given = (expand_in, project_in, squeeze_in, excite_in, depth_in)
    held = (expand, project, squeeze, excite, depth)
    moves = [pltpu.make_async_copy(a, b, sems.at[k]) for k, (a, b) in enumerate(zip(given, held))]
    for move in moves:
        move.start()
    rows, width = project.shape
    c_in = expand.shape[1]
    span = LANES - TAIL
    out[...] = jnp.zeros(out.shape, bf16)
    for move in moves:
        move.wait()
    out[0:rows, 0:width] = project[...]
    head = TAIL - exp
    out[0:rows, exp:TAIL] = expand[:, 0:head]

    def place(value, first):
        count = value.shape[0]
        spot = onehot(iota((count, span), 1) == iota((count, span), 0) + first)
        return dot(value, spot, TN)

    top, low = halves(depth[...])
    tail = place(squeeze[...].astype(bf16), sq)
    tail = tail + place(excite[...].astype(bf16), ex)
    tail = tail + place(top, dep) + place(low, dep + KS * KS)
    spot = onehot(iota((c_in, span), 0) == iota((c_in, span), 1) + head)
    tail = tail + dot(expand[...], spot)
    out[0:rows, TAIL:LANES] = tail.astype(bf16)


def trunk_kernel(
    plan, n_tokens,
    ids, cells_ref, film, learner, packed,
    tokens_out, mixed_out, attend_out, scale_out,
    w, e, d, h, wd, exw, sems,
):
    exp, sq, ex, dep = plan
    width = film.shape[2]
    hidden = packed.shape[0]
    late, early = (
        pltpu.make_async_copy(packed.at[:, lanes], w.at[:, lanes], sems.at[k])
        for k, lanes in enumerate((pl.ds(0, width), pl.ds(width, LANES - width)))
    )
    early.start()
    late.start()
    bands = GRID
    rows = bands * BAND
    n_frames = 3
    first = lax.axis_index("mp") * n_frames
    scales, shifts = [], []
    for f in range(n_frames):
        name = ids[first + f]
        row = film[name]
        scales.append(1.0 + row[0:1, :])
        shifts.append(row[1:2, :])

    def by_band(parts):
        frame = iota((BAND, parts[0].shape[1]), 0) % n_frames
        return jnp.where(frame == 0, parts[0], jnp.where(frame == 1, parts[1], parts[2]))

    scale_band = by_band(scales)
    shift_band = by_band(shifts)
    scale_out[...] = jnp.concatenate(scales + [jnp.zeros((8 - n_frames, width), f32)], axis=0)
    pick = (iota((16, LANES - TAIL), 1) == iota((16, LANES - TAIL), 0) + dep) | (
        iota((16, LANES - TAIL), 1) == iota((16, LANES - TAIL), 0) + dep + KS * KS
    )
    pick = onehot(pick & (iota((16, LANES - TAIL), 0) < KS * KS))
    early.wait()
    wd[...] = dot(pick, w[:, TAIL:LANES], NT)
    e[...] = dot(cells_ref[...], w[:, exp:exp + 256], NT)
    place = iota((BAND, 128), 0)
    has_left = place >= n_frames
    has_right = place < BAND - 2 - n_frames

    def chunk(j, carry):
        lanes = pl.ds(pl.multiple_of(j * 128, 128), 128)
        taps = [wd[t:t + 1, lanes] for t in range(KS * KS)]
        total = None
        done = None
        now = None

        def finish(r, value, total):
            out = swish(value)
            d[r * BAND:(r + 1) * BAND, lanes] = out
            return out if total is None else total + out

        for r in range(bands):
            mid = swish(e[r * BAND:(r + 1) * BAND, lanes])
            left = jnp.where(has_left, pltpu.roll(mid, n_frames, 0), 0.0)
            right = jnp.where(has_right, pltpu.roll(mid, BAND - n_frames, 0), 0.0)

            def taken(row):
                return (
                    taps[row * KS] * left + taps[row * KS + 1] * mid + taps[row * KS + 2] * right
                )

            if done is not None:
                total = finish(r - 1, done + taken(2), total)
            here = taken(1)
            if now is not None:
                here = here + now
            done, now = here, taken(0)
        total = finish(bands - 1, done, total)
        exw[:, lanes] = total
        return carry

    lax.fori_loop(0, hidden // 128, chunk, 0)
    member = (iota((8, BAND), 1) % n_frames == iota((8, BAND), 0)) & (
        iota((8, BAND), 1) < BAND - 2
    )
    mean = dot(onehot(member, f32), exw[...], precision=highest) * (1.0 / (GRID * GRID))
    top, low = halves(mean)
    stack = jnp.concatenate([top, low], axis=0)
    both = dot(stack, w[:, TAIL:LANES])
    reduced = both[0:8] + both[8:16]
    turned = pltpu.roll(swish(reduced), ex - sq, 1)
    lane = iota(turned.shape, 1)
    turned = jnp.where((lane >= ex) & (lane < dep), turned, 0.0)
    top, low = halves(turned)
    stack = jnp.concatenate([top, low], axis=0)
    both = dot(stack, w[:, TAIL:LANES], NT)
    excite = sigmoid(both[0:8] + both[8:16])
    exw[...] = by_band([excite[f:f + 1] for f in range(n_frames)])
    for r in range(bands):
        band = slice(r * BAND, (r + 1) * BAND)
        h[band, :] = (d[band, :] * exw[...]).astype(bf16)
    late.wait()
    block = dot(h[...], w[:, 0:width])
    mixed = (
        block.reshape(bands, BAND, width) * scale_band[None] + shift_band[None]
    ).reshape(rows, width)
    mixed_out[...] = mixed
    tiled = jnp.concatenate([learner[...]] * n_frames, axis=0)
    logits = dot(tiled, mixed, NT, highest)
    at = iota(logits.shape, 1) % BAND
    mine = (at % n_frames == iota(logits.shape, 0) // n_tokens) & (at < BAND - 2)
    attend = jnp.where(mine, sigmoid(logits), 0.0)
    attend_out[...] = attend
    tokens = dot(attend, mixed, precision=highest) * (1.0 / (GRID * GRID))
    tokens = tokens.astype(bf16)
    for k in range(tokens_out.shape[0]):
        tokens_out[k] = tokens


def slots_onehot(dest, peers, capacity):
    count = dest.shape[1]
    named = iota((peers, count), 0) == dest
    before = onehot(iota((count, count), 0) < iota((count, count), 1))
    ahead = dot(onehot(named), before)
    place = jnp.sum(jnp.where(named, ahead, 0.0), axis=0, keepdims=True)
    slot = dest * capacity + place.astype(jnp.int32)
    return onehot(iota((peers * capacity, count), 0) == slot)


def scatter_kernel(peers, capacity, tokens, dest, out):
    out[...] = dot(slots_onehot(dest[...], peers, capacity), tokens[...]).astype(bf16)


def pick_kernel(peers, capacity, arrived, dest, out):
    chosen = dot(slots_onehot(dest[...], peers, capacity), arrived[...], TN)
    each = out.shape[1]
    for k in range(out.shape[0]):
        out[k] = chosen[k * each:(k + 1) * each].astype(bf16)


def backward_kernel(n_tokens, cells, mixed, attend, scale, learner, grads, kept, sent, res):
    n_frames = 3
    share = kept.shape[1]
    grad = grads[0].astype(f32)
    for k in range(1, grads.shape[0]):
        grad = grad + grads[k].astype(f32)
    inner = dot(grad, mixed[...], NT, highest)
    held = attend[...]
    slope = inner * (1.0 / (GRID * GRID)) * held * (1.0 - held)
    both = jnp.concatenate([held * (1.0 / (GRID * GRID)), slope], axis=0)
    shape = (mixed.shape[0], n_frames * 128)
    row, lane = iota(shape, 0), iota(shape, 1)
    cell, frame = lane % 128, lane // 128
    spot = (row == cell // GRID * BAND + cell % GRID * n_frames + frame) & (cell < cells)
    both = dot(both, onehot(spot, f32), precision=highest)
    factors = jnp.concatenate([grad] + [learner[...]] * n_frames, axis=0)
    for f in range(n_frames):
        lanes = slice(f * 128, (f + 1) * 128)
        res[:, lanes] = dot(factors * scale[f:f + 1, :], both[:, lanes], TN, highest)
    me = lax.axis_index("mp")
    for k in range(kept.shape[0]):
        apart = 2 * sum(((k >> bit) & 1) << (2 - bit) for bit in range(3))
        for out, far in ((kept, apart), (sent, apart + 1)):
            first = pl.multiple_of(lax.bitwise_xor(me, far) * share, 8)
            out[k] = res[pl.ds(first, share), :].astype(bf16)


def join_kernel(wanted, *refs):
    *parts, out = refs
    for k, (part, block) in enumerate(wanted):
        out[k] = parts[part][block]


def settle_kernel(wanted, *refs):
    *parts, out = refs
    n_frames = 3
    cells = out.shape[2]
    me = lax.axis_index("mp")
    for k, (part, block) in enumerate(wanted):
        source = lax.bitwise_xor(me, k) * n_frames
        for f in range(n_frames):
            out[source + f] = parts[part][block, :, f * 128:f * 128 + cells]


def per_device(
    frames,
    instr_ids,
    film_table,
    w_expand,
    w_depth,
    w_squeeze,
    w_excite,
    w_project,
    w_learner,
    token_dest,
    w_policy,
    policy_cot,
):
    count, cells, c_in = frames.shape
    width = w_project.shape[1]
    n_tokens = w_learner.shape[1]
    n_mp = lax.axis_size("mp")
    peers = lax.axis_size("seq")
    capacity = policy_cot.shape[0] // peers
    share = width // n_mp
    n_frames = count // n_mp
    c_se = w_squeeze.shape[1]
    rows = GRID * BAND
    hidden = n_mp * SHARD
    plan = lane_plan(width, c_in, c_se)
    sds = jax.ShapeDtypeStruct
    vmem = pl.BlockSpec(memory_space=pltpu.VMEM)
    dest = token_dest.T
    learner = w_learner.T

    raw = (w_expand.T, w_project, w_squeeze.T, w_excite, w_depth)
    mine = call(
        functools.partial(pack_kernel, plan),
        sds((SHARD, LANES), bf16),
        *raw,
        in_specs=[pl.BlockSpec(memory_space=pl.ANY)] * len(raw),
        scratch=[pltpu.VMEM(a.shape, a.dtype) for a in raw]
        + [pltpu.SemaphoreType.DMA((len(raw),))],
        vmem=60,
    )
    across = [(m, m ^ 1) for m in range(n_mp)]
    packed = lax.all_gather(mine, "mp", axis=0, tiled=True)
    grad_part = dot(policy_cot, w_policy, NT).astype(bf16)
    arrived = lax.all_to_all(
        grad_part.reshape(peers, capacity, width), "seq", split_axis=0, concat_axis=0, tiled=True
    )
    picked = call(
        functools.partial(pick_kernel, peers, capacity),
        sds((n_mp, n_frames * n_tokens, width), bf16),
        arrived.reshape(peers * capacity, width), dest,
        flops=3e8, moved=2e6,
    )
    grads = lax.all_to_all(picked, "mp", split_axis=0, concat_axis=0, tiled=True)

    own = lax.dynamic_slice_in_dim(frames, lax.axis_index("mp") * n_frames, n_frames, 0)
    own = own.transpose(1, 0, 2).reshape(GRID, GRID * n_frames, c_in)
    own = jnp.pad(own, ((0, 0), (0, BAND - GRID * n_frames), (0, 256 - c_in)))
    own = own.reshape(rows, 256)
    copies, mixed, attend, scale = call(
        functools.partial(trunk_kernel, plan, n_tokens),
        (
            sds((n_mp, n_frames * n_tokens, width), bf16),
            sds((rows, width), f32),
            sds((n_frames * n_tokens, rows), f32),
            sds((8, width), f32),
        ),
        instr_ids, own, film_table, learner, packed,
        in_specs=[pl.BlockSpec(memory_space=pltpu.SMEM)] + [vmem] * 3 + [pl.BlockSpec(memory_space=pl.ANY)],
        scratch=[
            pltpu.VMEM((hidden, LANES), bf16),
            pltpu.VMEM((rows, hidden), f32),
            pltpu.VMEM((rows, hidden), f32),
            pltpu.VMEM((rows, hidden), bf16),
            pltpu.VMEM((16, hidden), f32),
            pltpu.VMEM((BAND, hidden), f32),
            pltpu.SemaphoreType.DMA((2,)),
        ],
        flops=2e9, moved=3e7, vmem=58,
    )
    tokens = lax.all_to_all(copies, "mp", split_axis=0, concat_axis=0, tiled=True)
    outgoing = call(
        functools.partial(scatter_kernel, peers, capacity),
        sds((peers * capacity, width), bf16),
        tokens.reshape(count * n_tokens, width), dest,
        flops=3e8, moved=2e6,
    )
    blocks = sds((n_mp // 2, share, n_frames * 128), bf16)
    kept, sent = call(
        functools.partial(backward_kernel, n_tokens, cells),
        (blocks, blocks),
        mixed, attend, scale, learner, grads,
        scratch=[pltpu.VMEM((width, n_frames * 128), f32)],
        flops=1e9, moved=2e6,
    )

    def swap(value, bit):
        return lax.ppermute(value, "mp", [(m, m ^ bit) for m in range(n_mp)])

    parts = [kept, swap(sent, 1)]
    groups = [(0, 0), (1, 0)]
    for step, bit in enumerate((2, 4, 8)):
        held = 4 >> step
        if bit == 4:
            outgoing, *parts = lax.optimization_barrier((outgoing, *parts))
        wanted = [(p, first + held + k) for p, first in groups for k in range(held)]
        sent = call(functools.partial(join_kernel, wanted), blocks, *parts)
        groups = groups + [(len(parts), held * k) for k in range(len(groups))]
        parts = parts + [swap(sent, bit)]
    rows_in = lax.all_to_all(
        outgoing.reshape(peers, capacity, width), "seq", split_axis=0, concat_axis=0, tiled=True
    )
    feature_grad = call(
        functools.partial(settle_kernel, groups), sds((count, share, cells), bf16), *parts
    )
    w_policy, feature_grad = lax.optimization_barrier((w_policy, feature_grad))
    policy_in = dot(rows_in.reshape(peers * capacity, width), w_policy).astype(bf16)

    feature_grad = feature_grad.transpose(0, 2, 1)
    return (policy_in, feature_grad)


def solution(mesh):
    return jax.shard_map(
        per_device,
        mesh=mesh,
        in_specs=(
            P("seq", None, None),
            P("seq"),
            P(),
            P(None, "mp"),
            P(None, "mp"),
            P("mp", None),
            P(None, "mp"),
            P("mp", None),
            P(),
            P("seq", None),
            P(None, "mp"),
            P("seq", "mp"),
        ),
        out_specs=(P("seq", "mp"), P("seq", None, "mp")),
        check_vma=False,
    )
```

```python
import functools

import jax
import jax.numpy as jnp
from jax import lax
from jax.experimental import pallas as pl
from jax.experimental.pallas import tpu as pltpu
from jax.sharding import PartitionSpec as P

KS = 3
GRID = 10
BAND = 32
SHARD = 88
LANES = 768
TAIL = 512
MIB = 1024 * 1024

highest = lax.Precision.HIGHEST
f32 = jnp.float32
bf16 = jnp.bfloat16

NN = (((1,), (0,)), ((), ()))
NT = (((1,), (1,)), ((), ()))
TN = (((0,), (0,)), ((), ()))


def dot(a, b, dims=NN, precision=None):
    return lax.dot_general(a, b, dims, precision=precision, preferred_element_type=f32)


def sigmoid(value):
    return 0.5 + 0.5 * jnp.tanh(0.5 * value)


def swish(value):
    half = 0.5 * value
    return half + half * jnp.tanh(half)


def iota(shape, dim):
    return lax.broadcasted_iota(jnp.int32, shape, dim)


def onehot(condition, dtype=bf16):
    return jnp.where(condition, 1.0, 0.0).astype(dtype)


def halves(value):
    top = value.astype(bf16)
    return top, (value - top.astype(f32)).astype(bf16)


def call(kernel, out_shape, *args, in_specs=None, scratch=(), flops=1e6, moved=1e6, vmem=12):
    return pl.pallas_call(
        kernel,
        out_shape=out_shape,
        in_specs=in_specs or [pl.BlockSpec(memory_space=pltpu.VMEM)] * len(args),
        out_specs=jax.tree.map(lambda _: pl.BlockSpec(memory_space=pltpu.VMEM), out_shape),
        scratch_shapes=scratch,
        compiler_params=pltpu.CompilerParams(vmem_limit_bytes=vmem * MIB),
        cost_estimate=pl.CostEstimate(
            flops=int(flops), bytes_accessed=int(moved), transcendentals=0
        ),
    )(*args)


def lane_plan(width, c_in, c_se):
    exp = width
    sq = exp + c_in
    ex = sq + c_se
    dep = ex + c_se
    return exp, sq - TAIL, ex - TAIL, dep - TAIL


def pack_kernel(
    plan, expand_in, project_in, squeeze_in, excite_in, depth_in, out,
    expand, project, squeeze, excite, depth, sems,
):
    exp, sq, ex, dep = plan
    given = (expand_in, project_in, squeeze_in, excite_in, depth_in)
    held = (expand, project, squeeze, excite, depth)
    moves = [pltpu.make_async_copy(a, b, sems.at[k]) for k, (a, b) in enumerate(zip(given, held))]
    for move in moves:
        move.start()
    rows, width = project.shape
    c_in = expand.shape[1]
    span = LANES - TAIL
    out[...] = jnp.zeros(out.shape, bf16)
    for move in moves:
        move.wait()
    out[0:rows, 0:width] = project[...]
    head = TAIL - exp
    out[0:rows, exp:TAIL] = expand[:, 0:head]

    def place(value, first):
        count = value.shape[0]
        spot = onehot(iota((count, span), 1) == iota((count, span), 0) + first)
        return dot(value, spot, TN)

    top, low = halves(depth[...])
    tail = place(squeeze[...].astype(bf16), sq)
    tail = tail + place(excite[...].astype(bf16), ex)
    tail = tail + place(top, dep) + place(low, dep + KS * KS)
    spot = onehot(iota((c_in, span), 0) == iota((c_in, span), 1) + head)
    tail = tail + dot(expand[...], spot)
    out[0:rows, TAIL:LANES] = tail.astype(bf16)


def trunk_kernel(
    plan, n_tokens,
    ids, own, table, learner_in, packed,
    tokens_out, carry_out,
    w, e, d, h, wd, exw, cells_ref, film, learner, sems,
):
    exp, sq, ex, dep = plan
    width = film.shape[2]
    hidden = packed.shape[0]
    bands = GRID
    rows = bands * BAND
    n_frames = 3
    first = lax.axis_index("mp") * n_frames
    front, back = pl.ds(0, width), pl.ds(width, LANES - width)
    pairs = [(packed.at[:, back], w.at[:, back]), (own, cells_ref), (learner_in, learner)]
    pairs += [(table.at[ids[first + f]], film.at[f]) for f in range(n_frames)]
    pairs += [(packed.at[:, front], w.at[:, front])]
    moves = [pltpu.make_async_copy(a, b, sems.at[k]) for k, (a, b) in enumerate(pairs)]
    for move in moves:
        move.start()
    for move in moves[:-1]:
        move.wait()
    scales = [1.0 + film[f, 0:1, :] for f in range(n_frames)]
    shifts = [film[f, 1:2, :] for f in range(n_frames)]

    def by_band(parts):
        frame = iota((BAND, parts[0].shape[1]), 0) % n_frames
        return jnp.where(frame == 0, parts[0], jnp.where(frame == 1, parts[1], parts[2]))

    scale_band = by_band(scales)
    shift_band = by_band(shifts)
    scale_out = jnp.concatenate(scales + [jnp.zeros((8 - n_frames, width), f32)], axis=0)
    carry_out[rows + n_frames * n_tokens:, :] = scale_out
    pick = (iota((16, LANES - TAIL), 1) == iota((16, LANES - TAIL), 0) + dep) | (
        iota((16, LANES - TAIL), 1) == iota((16, LANES - TAIL), 0) + dep + KS * KS
    )
    pick = onehot(pick & (iota((16, LANES - TAIL), 0) < KS * KS))
    wd[...] = dot(pick, w[:, TAIL:LANES], NT)
    e[...] = dot(cells_ref[...], w[:, exp:exp + 256], NT)
    place = iota((BAND, 128), 0)
    has_left = place >= n_frames
    has_right = place < BAND - 2 - n_frames

    def chunk(j, carry):
        lanes = pl.ds(pl.multiple_of(j * 128, 128), 128)
        taps = [wd[t:t + 1, lanes] for t in range(KS * KS)]
        total = None
        done = None
        now = None

        def finish(r, value, total):
            out = swish(value)
            d[r * BAND:(r + 1) * BAND, lanes] = out
            return out if total is None else total + out

        for r in range(bands):
            mid = swish(e[r * BAND:(r + 1) * BAND, lanes])
            left = jnp.where(has_left, pltpu.roll(mid, n_frames, 0), 0.0)
            right = jnp.where(has_right, pltpu.roll(mid, BAND - n_frames, 0), 0.0)

            def taken(row):
                return (
                    taps[row * KS] * left + taps[row * KS + 1] * mid + taps[row * KS + 2] * right
                )

            if done is not None:
                total = finish(r - 1, done + taken(2), total)
            here = taken(1)
            if now is not None:
                here = here + now
            done, now = here, taken(0)
        total = finish(bands - 1, done, total)
        exw[:, lanes] = total
        return carry

    lax.fori_loop(0, hidden // 128, chunk, 0)
    member = (iota((8, BAND), 1) % n_frames == iota((8, BAND), 0)) & (
        iota((8, BAND), 1) < BAND - 2
    )
    mean = dot(onehot(member, f32), exw[...], precision=highest) * (1.0 / (GRID * GRID))
    top, low = halves(mean)
    stack = jnp.concatenate([top, low], axis=0)
    both = dot(stack, w[:, TAIL:LANES])
    reduced = both[0:8] + both[8:16]
    turned = pltpu.roll(swish(reduced), ex - sq, 1)
    lane = iota(turned.shape, 1)
    turned = jnp.where((lane >= ex) & (lane < dep), turned, 0.0)
    top, low = halves(turned)
    stack = jnp.concatenate([top, low], axis=0)
    both = dot(stack, w[:, TAIL:LANES], NT)
    excite = sigmoid(both[0:8] + both[8:16])
    exw[...] = by_band([excite[f:f + 1] for f in range(n_frames)])
    for r in range(bands):
        band = slice(r * BAND, (r + 1) * BAND)
        h[band, :] = (d[band, :] * exw[...]).astype(bf16)
    moves[-1].wait()
    block = dot(h[...], w[:, 0:width])
    mixed = (
        block.reshape(bands, BAND, width) * scale_band[None] + shift_band[None]
    ).reshape(rows, width)
    carry_out[0:rows, :] = mixed
    tiled = jnp.concatenate([learner[...]] * n_frames, axis=0)
    logits = dot(tiled, mixed, NT, highest)
    at = iota(logits.shape, 1) % BAND
    mine = (at % n_frames == iota(logits.shape, 0) // n_tokens) & (at < BAND - 2)
    attend = jnp.where(mine, sigmoid(logits), 0.0)
    carry_out[rows:rows + n_frames * n_tokens, 0:rows] = attend
    tokens = dot(attend, mixed, precision=highest) * (1.0 / (GRID * GRID))
    tokens = tokens.astype(bf16)
    for k in range(tokens_out.shape[0]):
        tokens_out[k] = tokens


def slots_onehot(dest, peers, capacity):
    count = dest.shape[1]
    named = iota((peers, count), 0) == dest
    before = onehot(iota((count, count), 0) < iota((count, count), 1))
    ahead = dot(onehot(named), before)
    place = jnp.sum(jnp.where(named, ahead, 0.0), axis=0, keepdims=True)
    slot = dest * capacity + place.astype(jnp.int32)
    return onehot(iota((peers * capacity, count), 0) == slot)


def scatter_kernel(peers, capacity, tokens, dest, after, out):
    del after
    out[...] = dot(slots_onehot(dest[...], peers, capacity), tokens[...]).astype(bf16)


def pick_kernel(peers, capacity, arrived, dest, out):
    chosen = dot(slots_onehot(dest[...], peers, capacity), arrived[...], TN)
    each = out.shape[1]
    for k in range(out.shape[0]):
        out[k] = chosen[k * each:(k + 1) * each].astype(bf16)


def backward_kernel(n_tokens, cells, carry, learner, grads, *outs):
    n_frames = 3
    *far, res = outs
    share = far[0].shape[1]
    rows = GRID * BAND
    mixed = carry[0:rows, :]
    held = carry[rows:rows + n_frames * n_tokens, 0:rows]
    scale = carry[rows + n_frames * n_tokens:, :]
    grad = grads[0].astype(f32)
    for k in range(1, grads.shape[0]):
        grad = grad + grads[k].astype(f32)
    inner = dot(grad, mixed, NT, highest)
    slope = inner * (1.0 / (GRID * GRID)) * held * (1.0 - held)
    both = jnp.concatenate([held * (1.0 / (GRID * GRID)), slope], axis=0)
    shape = (mixed.shape[0], n_frames * 128)
    row, lane = iota(shape, 0), iota(shape, 1)
    cell, frame = lane % 128, lane // 128
    spot = (row == cell // GRID * BAND + cell % GRID * n_frames + frame) & (cell < cells)
    both = dot(both, onehot(spot, f32), precision=highest)
    factors = jnp.concatenate([grad] + [learner[...]] * n_frames, axis=0)
    for f in range(n_frames):
        lanes = slice(f * 128, (f + 1) * 128)
        res[:, lanes] = dot(factors * scale[f:f + 1, :], both[:, lanes], TN, highest)
    me = lax.axis_index("mp")
    for k, out in enumerate(far):
        near = out.shape[0]
        for j in range(near):
            first = pl.multiple_of(lax.bitwise_xor(me, near * k + j) * share, 8)
            out[j] = res[pl.ds(first, share), :].astype(bf16)


def join_kernel(after, *refs):
    del after
    parts, outs = refs[:len(refs) // 2 + 1], refs[len(refs) // 2 + 1:]
    for j, out in enumerate(outs):
        for k, part in enumerate(parts):
            out[k] = part[j + 1]


def settle_kernel(*refs):
    *parts, out = refs
    n_frames = 3
    cells = out.shape[2]
    me = lax.axis_index("mp")
    near = parts[0].shape[0]
    far, joined = parts[:len(parts) - near + 1], parts[len(parts) - near + 1:]
    for k in range(len(far)):
        for j in range(near):
            block = far[k][0] if j == 0 else joined[j - 1][k]
            source = lax.bitwise_xor(me, near * k + j) * n_frames
            for f in range(n_frames):
                out[source + f] = block[:, f * 128:f * 128 + cells]


def per_device(
    frames,
    instr_ids,
    film_table,
    w_expand,
    w_depth,
    w_squeeze,
    w_excite,
    w_project,
    w_learner,
    token_dest,
    w_policy,
    policy_cot,
):
    count, cells, c_in = frames.shape
    width = w_project.shape[1]
    n_tokens = w_learner.shape[1]
    n_mp = lax.axis_size("mp")
    peers = lax.axis_size("seq")
    capacity = policy_cot.shape[0] // peers
    share = width // n_mp
    n_frames = count // n_mp
    c_se = w_squeeze.shape[1]
    rows = GRID * BAND
    hidden = n_mp * SHARD
    plan = lane_plan(width, c_in, c_se)
    sds = jax.ShapeDtypeStruct
    vmem = pl.BlockSpec(memory_space=pltpu.VMEM)
    dest = token_dest.T
    learner = w_learner.T

    raw = (w_expand.T, w_project, w_squeeze.T, w_excite, w_depth)
    mine = call(
        functools.partial(pack_kernel, plan),
        sds((SHARD, LANES), bf16),
        *raw,
        in_specs=[pl.BlockSpec(memory_space=pl.ANY)] * len(raw),
        scratch=[pltpu.VMEM(a.shape, a.dtype) for a in raw]
        + [pltpu.SemaphoreType.DMA((len(raw),))],
        vmem=60,
    )
    across = [(m, m ^ 1) for m in range(n_mp)]
    packed = lax.all_gather(mine, "mp", axis=0, tiled=True)
    grad_part = dot(policy_cot, w_policy, NT).astype(bf16)
    arrived = lax.all_to_all(
        grad_part.reshape(peers, capacity, width), "seq", split_axis=0, concat_axis=0, tiled=True
    )
    picked = call(
        functools.partial(pick_kernel, peers, capacity),
        sds((n_mp, n_frames * n_tokens, width), bf16),
        arrived.reshape(peers * capacity, width), dest,
        flops=3e8, moved=2e6,
    )
    grads = lax.all_to_all(picked, "mp", split_axis=0, concat_axis=0, tiled=True)

    packed, grads = lax.optimization_barrier((packed, grads))
    own = lax.dynamic_slice_in_dim(frames, lax.axis_index("mp") * n_frames, n_frames, 0)
    own = own.transpose(1, 0, 2).reshape(GRID, GRID * n_frames, c_in)
    own = jnp.pad(own, ((0, 0), (0, BAND - GRID * n_frames), (0, 256 - c_in)))
    own = own.reshape(rows, 256)
    copies, carry = call(
        functools.partial(trunk_kernel, plan, n_tokens),
        (
            sds((n_mp, n_frames * n_tokens, width), bf16),
            sds((rows + n_frames * n_tokens + 8, width), f32),
        ),
        instr_ids, own, film_table, learner, packed,
        in_specs=[pl.BlockSpec(memory_space=pltpu.SMEM)] + [pl.BlockSpec(memory_space=pl.ANY)] * 4,
        scratch=[
            pltpu.VMEM((hidden, LANES), bf16),
            pltpu.VMEM((rows, hidden), f32),
            pltpu.VMEM((rows, hidden), f32),
            pltpu.VMEM((rows, hidden), bf16),
            pltpu.VMEM((16, hidden), f32),
            pltpu.VMEM((BAND, hidden), f32),
            pltpu.VMEM((rows, 256), bf16),
            pltpu.VMEM((n_frames, 2, width), f32),
            pltpu.VMEM((n_tokens, width), f32),
            pltpu.SemaphoreType.DMA((4 + n_frames,)),
        ],
        flops=2e9, moved=3e7, vmem=58,
    )
    tokens = lax.all_to_all(copies, "mp", split_axis=0, concat_axis=0, tiled=True)
    near = 4
    blocks = sds((near, share, n_frames * 128), bf16)
    parts = call(
        functools.partial(backward_kernel, n_tokens, cells),
        (blocks,) * (n_mp // near),
        carry, learner, grads,
        scratch=[pltpu.VMEM((width, n_frames * 128), f32)],
        flops=1e9, moved=2e6,
    )

    def swap(value, far):
        return lax.ppermute(value, "mp", [(m, m ^ far) for m in range(n_mp)]) if far else value

    parts = [swap(part, near * k) for k, part in enumerate(parts)]
    outgoing = call(
        functools.partial(scatter_kernel, peers, capacity),
        sds((peers * capacity, width), bf16),
        tokens.reshape(count * n_tokens, width), dest, parts[2],
        in_specs=[vmem, vmem, pl.BlockSpec(memory_space=pl.ANY)],
        flops=3e8, moved=2e6,
    )
    joined = call(join_kernel, (blocks,) * (near - 1), outgoing, *parts,
                  in_specs=[pl.BlockSpec(memory_space=pl.ANY)] + [vmem] * len(parts))
    joined = [swap(part, j + 1) for j, part in enumerate(joined)]
    rows_in = lax.all_to_all(
        outgoing.reshape(peers, capacity, width), "seq", split_axis=0, concat_axis=0, tiled=True
    )
    feature_grad = call(settle_kernel, sds((count, share, cells), bf16), *parts, *joined)
    rows_in, feature_grad = lax.optimization_barrier((rows_in, feature_grad))
    policy_in = dot(rows_in.reshape(peers * capacity, width), w_policy).astype(bf16)

    feature_grad = feature_grad.transpose(0, 2, 1)
    return (policy_in, feature_grad)


def solution(mesh):
    return jax.shard_map(
        per_device,
        mesh=mesh,
        in_specs=(
            P("seq", None, None),
            P("seq"),
            P(),
            P(None, "mp"),
            P(None, "mp"),
            P("mp", None),
            P(None, "mp"),
            P("mp", None),
            P(),
            P("seq", None),
            P(None, "mp"),
            P("seq", "mp"),
        ),
        out_specs=(P("seq", "mp"), P("seq", None, "mp")),
        check_vma=False,
    )
```

```python
import functools

import jax
import jax.numpy as jnp
from jax import lax
from jax.experimental import pallas as pl
from jax.experimental.pallas import tpu as pltpu
from jax.sharding import PartitionSpec as P

KS = 3
GRID = 10
BAND = 32
SHARD = 88
LANES = 768
TAIL = 512
MIB = 1024 * 1024

highest = lax.Precision.HIGHEST
f32 = jnp.float32
bf16 = jnp.bfloat16

NN = (((1,), (0,)), ((), ()))
NT = (((1,), (1,)), ((), ()))
TN = (((0,), (0,)), ((), ()))


def dot(a, b, dims=NN, precision=None):
    return lax.dot_general(a, b, dims, precision=precision, preferred_element_type=f32)


def sigmoid(value):
    return 0.5 + 0.5 * jnp.tanh(0.5 * value)


def swish(value):
    half = 0.5 * value
    return half + half * jnp.tanh(half)


def iota(shape, dim):
    return lax.broadcasted_iota(jnp.int32, shape, dim)


def onehot(condition, dtype=bf16):
    return jnp.where(condition, 1.0, 0.0).astype(dtype)


def halves(value):
    top = value.astype(bf16)
    return top, (value - top.astype(f32)).astype(bf16)


def call(kernel, out_shape, *args, in_specs=None, scratch=(), flops=1e6, moved=1e6, vmem=12):
    return pl.pallas_call(
        kernel,
        out_shape=out_shape,
        in_specs=in_specs or [pl.BlockSpec(memory_space=pltpu.VMEM)] * len(args),
        out_specs=jax.tree.map(lambda _: pl.BlockSpec(memory_space=pltpu.VMEM), out_shape),
        scratch_shapes=scratch,
        compiler_params=pltpu.CompilerParams(vmem_limit_bytes=vmem * MIB),
        cost_estimate=pl.CostEstimate(
            flops=int(flops), bytes_accessed=int(moved), transcendentals=0
        ),
    )(*args)


def lane_plan(width, c_in, c_se):
    exp = width
    sq = exp + c_in
    ex = sq + c_se
    dep = ex + c_se
    return exp, sq - TAIL, ex - TAIL, dep - TAIL


def pack_kernel(
    plan, expand_in, project_in, squeeze_in, excite_in, depth_in, out,
    expand, project, squeeze, excite, depth, sems,
):
    exp, sq, ex, dep = plan
    given = (expand_in, project_in, squeeze_in, excite_in, depth_in)
    held = (expand, project, squeeze, excite, depth)
    moves = [pltpu.make_async_copy(a, b, sems.at[k]) for k, (a, b) in enumerate(zip(given, held))]
    for move in moves:
        move.start()
    rows, width = project.shape
    c_in = expand.shape[1]
    span = LANES - TAIL
    out[...] = jnp.zeros(out.shape, bf16)
    for move in moves:
        move.wait()
    out[0:rows, 0:width] = project[...]
    head = TAIL - exp
    out[0:rows, exp:TAIL] = expand[:, 0:head]

    def place(value, first):
        count = value.shape[0]
        spot = onehot(iota((count, span), 1) == iota((count, span), 0) + first)
        return dot(value, spot, TN)

    top, low = halves(depth[...])
    tail = place(squeeze[...].astype(bf16), sq)
    tail = tail + place(excite[...].astype(bf16), ex)
    tail = tail + place(top, dep) + place(low, dep + KS * KS)
    spot = onehot(iota((c_in, span), 0) == iota((c_in, span), 1) + head)
    tail = tail + dot(expand[...], spot)
    out[0:rows, TAIL:LANES] = tail.astype(bf16)


def trunk_kernel(
    plan, n_tokens,
    ids, own, table, learner_in, packed, after,
    tokens_out, carry_out,
    w, e, d, h, wd, exw, cells_ref, film, learner, sems,
):
    del after
    exp, sq, ex, dep = plan
    width = film.shape[2]
    hidden = packed.shape[0]
    bands = GRID
    rows = bands * BAND
    n_frames = 3
    first = lax.axis_index("mp") * n_frames
    front, back = pl.ds(0, width), pl.ds(width, LANES - width)
    pairs = [(packed.at[:, back], w.at[:, back]), (own, cells_ref), (learner_in, learner)]
    pairs += [(table.at[ids[first + f]], film.at[f]) for f in range(n_frames)]
    pairs += [(packed.at[:, front], w.at[:, front])]
    moves = [pltpu.make_async_copy(a, b, sems.at[k]) for k, (a, b) in enumerate(pairs)]
    for move in moves:
        move.start()
    for move in moves[:-1]:
        move.wait()
    scales = [1.0 + film[f, 0:1, :] for f in range(n_frames)]
    shifts = [film[f, 1:2, :] for f in range(n_frames)]

    def by_band(parts):
        frame = iota((BAND, parts[0].shape[1]), 0) % n_frames
        return jnp.where(frame == 0, parts[0], jnp.where(frame == 1, parts[1], parts[2]))

    scale_band = by_band(scales)
    shift_band = by_band(shifts)
    scale_out = jnp.concatenate(scales + [jnp.zeros((8 - n_frames, width), f32)], axis=0)
    carry_out[rows + n_frames * n_tokens:, :] = scale_out
    pick = (iota((16, LANES - TAIL), 1) == iota((16, LANES - TAIL), 0) + dep) | (
        iota((16, LANES - TAIL), 1) == iota((16, LANES - TAIL), 0) + dep + KS * KS
    )
    pick = onehot(pick & (iota((16, LANES - TAIL), 0) < KS * KS))
    wd[...] = dot(pick, w[:, TAIL:LANES], NT)
    e[...] = dot(cells_ref[...], w[:, exp:exp + 256], NT)
    place = iota((BAND, 128), 0)
    has_left = place >= n_frames
    has_right = place < BAND - 2 - n_frames

    def chunk(j, carry):
        lanes = pl.ds(pl.multiple_of(j * 128, 128), 128)
        taps = [wd[t:t + 1, lanes] for t in range(KS * KS)]
        total = None
        done = None
        now = None

        def finish(r, value, total):
            out = swish(value)
            d[r * BAND:(r + 1) * BAND, lanes] = out
            return out if total is None else total + out

        for r in range(bands):
            mid = swish(e[r * BAND:(r + 1) * BAND, lanes])
            left = jnp.where(has_left, pltpu.roll(mid, n_frames, 0), 0.0)
            right = jnp.where(has_right, pltpu.roll(mid, BAND - n_frames, 0), 0.0)

            def taken(row):
                return (
                    taps[row * KS] * left + taps[row * KS + 1] * mid + taps[row * KS + 2] * right
                )

            if done is not None:
                total = finish(r - 1, done + taken(2), total)
            here = taken(1)
            if now is not None:
                here = here + now
            done, now = here, taken(0)
        total = finish(bands - 1, done, total)
        exw[:, lanes] = total
        return carry

    lax.fori_loop(0, hidden // 128, chunk, 0)
    member = (iota((8, BAND), 1) % n_frames == iota((8, BAND), 0)) & (
        iota((8, BAND), 1) < BAND - 2
    )
    mean = dot(onehot(member, f32), exw[...], precision=highest) * (1.0 / (GRID * GRID))
    top, low = halves(mean)
    stack = jnp.concatenate([top, low], axis=0)
    both = dot(stack, w[:, TAIL:LANES])
    reduced = both[0:8] + both[8:16]
    turned = pltpu.roll(swish(reduced), ex - sq, 1)
    lane = iota(turned.shape, 1)
    turned = jnp.where((lane >= ex) & (lane < dep), turned, 0.0)
    top, low = halves(turned)
    stack = jnp.concatenate([top, low], axis=0)
    both = dot(stack, w[:, TAIL:LANES], NT)
    excite = sigmoid(both[0:8] + both[8:16])
    exw[...] = by_band([excite[f:f + 1] for f in range(n_frames)])
    for r in range(bands):
        band = slice(r * BAND, (r + 1) * BAND)
        h[band, :] = (d[band, :] * exw[...]).astype(bf16)
    moves[-1].wait()
    block = dot(h[...], w[:, 0:width])
    mixed = (
        block.reshape(bands, BAND, width) * scale_band[None] + shift_band[None]
    ).reshape(rows, width)
    carry_out[0:rows, :] = mixed
    tiled = jnp.concatenate([learner[...]] * n_frames, axis=0)
    logits = dot(tiled, mixed, NT, highest)
    at = iota(logits.shape, 1) % BAND
    mine = (at % n_frames == iota(logits.shape, 0) // n_tokens) & (at < BAND - 2)
    attend = jnp.where(mine, sigmoid(logits), 0.0)
    carry_out[rows:rows + n_frames * n_tokens, 0:rows] = attend
    tokens = dot(attend, mixed, precision=highest) * (1.0 / (GRID * GRID))
    tokens = tokens.astype(bf16)
    for k in range(tokens_out.shape[0]):
        tokens_out[k] = tokens


def slots_onehot(dest, peers, capacity):
    count = dest.shape[1]
    named = iota((peers, count), 0) == dest
    before = onehot(iota((count, count), 0) < iota((count, count), 1))
    ahead = dot(onehot(named), before)
    place = jnp.sum(jnp.where(named, ahead, 0.0), axis=0, keepdims=True)
    slot = dest * capacity + place.astype(jnp.int32)
    return onehot(iota((peers * capacity, count), 0) == slot)


def scatter_kernel(peers, capacity, tokens, dest, after, out):
    del after
    out[...] = dot(slots_onehot(dest[...], peers, capacity), tokens[...]).astype(bf16)


def pick_kernel(peers, capacity, arrived, dest, out):
    chosen = dot(slots_onehot(dest[...], peers, capacity), arrived[...], TN)
    each = out.shape[1]
    for k in range(out.shape[0]):
        out[k] = chosen[k * each:(k + 1) * each].astype(bf16)


def backward_kernel(n_tokens, cells, carry, learner, grads, *outs):
    n_frames = 3
    *far, res = outs
    share = far[0].shape[1]
    rows = GRID * BAND
    mixed = carry[0:rows, :]
    held = carry[rows:rows + n_frames * n_tokens, 0:rows]
    scale = carry[rows + n_frames * n_tokens:, :]
    grad = grads[0].astype(f32)
    for k in range(1, grads.shape[0]):
        grad = grad + grads[k].astype(f32)
    inner = dot(grad, mixed, NT, highest)
    slope = inner * (1.0 / (GRID * GRID)) * held * (1.0 - held)
    both = jnp.concatenate([held * (1.0 / (GRID * GRID)), slope], axis=0)
    shape = (mixed.shape[0], n_frames * 128)
    row, lane = iota(shape, 0), iota(shape, 1)
    cell, frame = lane % 128, lane // 128
    spot = (row == cell // GRID * BAND + cell % GRID * n_frames + frame) & (cell < cells)
    both = dot(both, onehot(spot, f32), precision=highest)
    factors = jnp.concatenate([grad] + [learner[...]] * n_frames, axis=0)
    for f in range(n_frames):
        lanes = slice(f * 128, (f + 1) * 128)
        res[:, lanes] = dot(factors * scale[f:f + 1, :], both[:, lanes], TN, highest)
    me = lax.axis_index("mp")
    for k, out in enumerate(far):
        near = out.shape[0]
        for j in range(near):
            first = pl.multiple_of(lax.bitwise_xor(me, near * k + j) * share, 8)
            out[j] = res[pl.ds(first, share), :].astype(bf16)


def join_kernel(after, *refs):
    del after
    parts, outs = refs[:len(refs) // 2 + 1], refs[len(refs) // 2 + 1:]
    for j, out in enumerate(outs):
        for k, part in enumerate(parts):
            out[k] = part[j + 1]


def settle_kernel(*refs):
    *parts, out = refs
    n_frames = 3
    cells = out.shape[2]
    me = lax.axis_index("mp")
    near = parts[0].shape[0]
    far, joined = parts[:len(parts) - near + 1], parts[len(parts) - near + 1:]
    for k in range(len(far)):
        for j in range(near):
            block = far[k][0] if j == 0 else joined[j - 1][k]
            source = lax.bitwise_xor(me, near * k + j) * n_frames
            for f in range(n_frames):
                out[source + f] = block[:, f * 128:f * 128 + cells]


def per_device(
    frames,
    instr_ids,
    film_table,
    w_expand,
    w_depth,
    w_squeeze,
    w_excite,
    w_project,
    w_learner,
    token_dest,
    w_policy,
    policy_cot,
):
    count, cells, c_in = frames.shape
    width = w_project.shape[1]
    n_tokens = w_learner.shape[1]
    n_mp = lax.axis_size("mp")
    peers = lax.axis_size("seq")
    capacity = policy_cot.shape[0] // peers
    share = width // n_mp
    n_frames = count // n_mp
    c_se = w_squeeze.shape[1]
    rows = GRID * BAND
    hidden = n_mp * SHARD
    plan = lane_plan(width, c_in, c_se)
    sds = jax.ShapeDtypeStruct
    vmem = pl.BlockSpec(memory_space=pltpu.VMEM)
    dest = token_dest.T
    learner = w_learner.T

    raw = (w_expand.T, w_project, w_squeeze.T, w_excite, w_depth)
    mine = call(
        functools.partial(pack_kernel, plan),
        sds((SHARD, LANES), bf16),
        *raw,
        in_specs=[pl.BlockSpec(memory_space=pl.ANY)] * len(raw),
        scratch=[pltpu.VMEM(a.shape, a.dtype) for a in raw]
        + [pltpu.SemaphoreType.DMA((len(raw),))],
        vmem=60,
    )
    across = [(m, m ^ 1) for m in range(n_mp)]
    packed = lax.all_gather(mine, "mp", axis=0, tiled=True)
    grad_part = dot(policy_cot, w_policy, NT).astype(bf16)
    arrived = lax.all_to_all(
        grad_part.reshape(peers, capacity, width), "seq", split_axis=0, concat_axis=0, tiled=True
    )
    picked = call(
        functools.partial(pick_kernel, peers, capacity),
        sds((n_mp, n_frames * n_tokens, width), bf16),
        arrived.reshape(peers * capacity, width), dest,
        flops=3e8, moved=2e6,
    )
    grads = lax.all_to_all(picked, "mp", split_axis=0, concat_axis=0, tiled=True)

    own = lax.dynamic_slice_in_dim(frames, lax.axis_index("mp") * n_frames, n_frames, 0)
    own = own.transpose(1, 0, 2).reshape(GRID, GRID * n_frames, c_in)
    own = jnp.pad(own, ((0, 0), (0, BAND - GRID * n_frames), (0, 256 - c_in)))
    own = own.reshape(rows, 256)
    copies, carry = call(
        functools.partial(trunk_kernel, plan, n_tokens),
        (
            sds((n_mp, n_frames * n_tokens, width), bf16),
            sds((rows + n_frames * n_tokens + 8, width), f32),
        ),
        instr_ids, own, film_table, learner, packed, picked,
        in_specs=[pl.BlockSpec(memory_space=pltpu.SMEM)] + [pl.BlockSpec(memory_space=pl.ANY)] * 5,
        scratch=[
            pltpu.VMEM((hidden, LANES), bf16),
            pltpu.VMEM((rows, hidden), f32),
            pltpu.VMEM((rows, hidden), f32),
            pltpu.VMEM((rows, hidden), bf16),
            pltpu.VMEM((16, hidden), f32),
            pltpu.VMEM((BAND, hidden), f32),
            pltpu.VMEM((rows, 256), bf16),
            pltpu.VMEM((n_frames, 2, width), f32),
            pltpu.VMEM((n_tokens, width), f32),
            pltpu.SemaphoreType.DMA((4 + n_frames,)),
        ],
        flops=2e9, moved=3e7, vmem=58,
    )
    tokens = lax.all_to_all(copies, "mp", split_axis=0, concat_axis=0, tiled=True)
    near = 4
    blocks = sds((near, share, n_frames * 128), bf16)
    parts = call(
        functools.partial(backward_kernel, n_tokens, cells),
        (blocks,) * (n_mp // near),
        carry, learner, grads,
        scratch=[pltpu.VMEM((width, n_frames * 128), f32)],
        flops=1e9, moved=2e6,
    )

    def swap(value, far):
        return lax.ppermute(value, "mp", [(m, m ^ far) for m in range(n_mp)]) if far else value

    parts = [swap(part, near * k) for k, part in enumerate(parts)]
    outgoing = call(
        functools.partial(scatter_kernel, peers, capacity),
        sds((peers * capacity, width), bf16),
        tokens.reshape(count * n_tokens, width), dest, parts[1],
        in_specs=[vmem, vmem, pl.BlockSpec(memory_space=pl.ANY)],
        flops=3e8, moved=2e6,
    )
    joined = call(join_kernel, (blocks,) * (near - 1), outgoing, *parts,
                  in_specs=[pl.BlockSpec(memory_space=pl.ANY)] + [vmem] * len(parts))
    joined = [swap(part, j + 1) for j, part in enumerate(joined)]
    rows_in = lax.all_to_all(
        outgoing.reshape(peers, capacity, width), "seq", split_axis=0, concat_axis=0, tiled=True
    )
    feature_grad = call(settle_kernel, sds((count, share, cells), bf16), *parts, *joined)
    rows_in, feature_grad = lax.optimization_barrier((rows_in, feature_grad))
    policy_in = dot(rows_in.reshape(peers * capacity, width), w_policy).astype(bf16)

    feature_grad = feature_grad.transpose(0, 2, 1)
    return (policy_in, feature_grad)


def solution(mesh):
    return jax.shard_map(
        per_device,
        mesh=mesh,
        in_specs=(
            P("seq", None, None),
            P("seq"),
            P(),
            P(None, "mp"),
            P(None, "mp"),
            P("mp", None),
            P(None, "mp"),
            P("mp", None),
            P(),
            P("seq", None),
            P(None, "mp"),
            P("seq", "mp"),
        ),
        out_specs=(P("seq", "mp"), P("seq", None, "mp")),
        check_vma=False,
    )
```

```python
import functools

import jax
import jax.numpy as jnp
from jax import lax
from jax.experimental import pallas as pl
from jax.experimental.pallas import tpu as pltpu
from jax.sharding import PartitionSpec as P

KS = 3
GRID = 10
BAND = 32
SHARD = 88
LANES = 768
TAIL = 512
MIB = 1024 * 1024

highest = lax.Precision.HIGHEST
f32 = jnp.float32
bf16 = jnp.bfloat16

NN = (((1,), (0,)), ((), ()))
NT = (((1,), (1,)), ((), ()))
TN = (((0,), (0,)), ((), ()))


def dot(a, b, dims=NN, precision=None):
    return lax.dot_general(a, b, dims, precision=precision, preferred_element_type=f32)


def sigmoid(value):
    return 0.5 + 0.5 * jnp.tanh(0.5 * value)


def swish(value):
    half = 0.5 * value
    return half + half * jnp.tanh(half)


def iota(shape, dim):
    return lax.broadcasted_iota(jnp.int32, shape, dim)


def onehot(condition, dtype=bf16):
    return jnp.where(condition, 1.0, 0.0).astype(dtype)


def halves(value):
    top = value.astype(bf16)
    return top, (value - top.astype(f32)).astype(bf16)


def call(kernel, out_shape, *args, in_specs=None, scratch=(), flops=1e6, moved=1e6, vmem=12):
    return pl.pallas_call(
        kernel,
        out_shape=out_shape,
        in_specs=in_specs or [pl.BlockSpec(memory_space=pltpu.VMEM)] * len(args),
        out_specs=jax.tree.map(lambda _: pl.BlockSpec(memory_space=pltpu.VMEM), out_shape),
        scratch_shapes=scratch,
        compiler_params=pltpu.CompilerParams(vmem_limit_bytes=vmem * MIB),
        cost_estimate=pl.CostEstimate(
            flops=int(flops), bytes_accessed=int(moved), transcendentals=0
        ),
    )(*args)


def lane_plan(width, c_in, c_se):
    exp = width
    sq = exp + c_in
    ex = sq + c_se
    dep = ex + c_se
    return exp, sq - TAIL, ex - TAIL, dep - TAIL


def pack_kernel(
    plan, expand_in, project_in, squeeze_in, excite_in, depth_in, out,
    expand, project, squeeze, excite, depth, sems,
):
    exp, sq, ex, dep = plan
    given = (expand_in, project_in, squeeze_in, excite_in, depth_in)
    held = (expand, project, squeeze, excite, depth)
    moves = [pltpu.make_async_copy(a, b, sems.at[k]) for k, (a, b) in enumerate(zip(given, held))]
    for move in moves:
        move.start()
    rows, width = project.shape
    c_in = expand.shape[1]
    span = LANES - TAIL
    out[...] = jnp.zeros(out.shape, bf16)
    for move in moves:
        move.wait()
    out[0:rows, 0:width] = project[...]
    head = TAIL - exp
    out[0:rows, exp:TAIL] = expand[:, 0:head]

    def place(value, first):
        count = value.shape[0]
        spot = onehot(iota((count, span), 1) == iota((count, span), 0) + first)
        return dot(value, spot, TN)

    top, low = halves(depth[...])
    tail = place(squeeze[...].astype(bf16), sq)
    tail = tail + place(excite[...].astype(bf16), ex)
    tail = tail + place(top, dep) + place(low, dep + KS * KS)
    spot = onehot(iota((c_in, span), 0) == iota((c_in, span), 1) + head)
    tail = tail + dot(expand[...], spot)
    out[0:rows, TAIL:LANES] = tail.astype(bf16)


def trunk_kernel(
    plan, n_tokens,
    ids, own, table, learner_in, packed, after,
    tokens_out, carry_out,
    w, e, d, h, wd, exw, cells_ref, film, learner, sems,
):
    del after
    exp, sq, ex, dep = plan
    width = film.shape[2]
    hidden = packed.shape[0]
    bands = GRID
    rows = bands * BAND
    n_frames = 3
    first = lax.axis_index("mp") * n_frames
    front, back = pl.ds(0, width), pl.ds(width, LANES - width)
    pairs = [(packed.at[:, back], w.at[:, back]), (own, cells_ref), (learner_in, learner)]
    pairs += [(table.at[ids[first + f]], film.at[f]) for f in range(n_frames)]
    pairs += [(packed.at[:, front], w.at[:, front])]
    moves = [pltpu.make_async_copy(a, b, sems.at[k]) for k, (a, b) in enumerate(pairs)]
    for move in moves:
        move.start()
    for move in moves[:-1]:
        move.wait()
    scales = [1.0 + film[f, 0:1, :] for f in range(n_frames)]
    shifts = [film[f, 1:2, :] for f in range(n_frames)]

    def by_band(parts):
        frame = iota((BAND, parts[0].shape[1]), 0) % n_frames
        return jnp.where(frame == 0, parts[0], jnp.where(frame == 1, parts[1], parts[2]))

    scale_band = by_band(scales)
    shift_band = by_band(shifts)
    scale_out = jnp.concatenate(scales + [jnp.zeros((8 - n_frames, width), f32)], axis=0)
    carry_out[rows + n_frames * n_tokens:, :] = scale_out
    pick = (iota((16, LANES - TAIL), 1) == iota((16, LANES - TAIL), 0) + dep) | (
        iota((16, LANES - TAIL), 1) == iota((16, LANES - TAIL), 0) + dep + KS * KS
    )
    pick = onehot(pick & (iota((16, LANES - TAIL), 0) < KS * KS))
    wd[...] = dot(pick, w[:, TAIL:LANES], NT)
    e[...] = dot(cells_ref[...], w[:, exp:exp + 256], NT)
    place = iota((BAND, 128), 0)
    has_left = place >= n_frames
    has_right = place < BAND - 2 - n_frames

    def chunk(j, carry):
        lanes = pl.ds(pl.multiple_of(j * 128, 128), 128)
        taps = [wd[t:t + 1, lanes] for t in range(KS * KS)]
        total = None
        done = None
        now = None

        def finish(r, value, total):
            out = swish(value)
            d[r * BAND:(r + 1) * BAND, lanes] = out
            return out if total is None else total + out

        for r in range(bands):
            mid = swish(e[r * BAND:(r + 1) * BAND, lanes])
            left = jnp.where(has_left, pltpu.roll(mid, n_frames, 0), 0.0)
            right = jnp.where(has_right, pltpu.roll(mid, BAND - n_frames, 0), 0.0)

            def taken(row):
                return (
                    taps[row * KS] * left + taps[row * KS + 1] * mid + taps[row * KS + 2] * right
                )

            if done is not None:
                total = finish(r - 1, done + taken(2), total)
            here = taken(1)
            if now is not None:
                here = here + now
            done, now = here, taken(0)
        total = finish(bands - 1, done, total)
        exw[:, lanes] = total
        return carry

    lax.fori_loop(0, hidden // 128, chunk, 0)
    member = (iota((8, BAND), 1) % n_frames == iota((8, BAND), 0)) & (
        iota((8, BAND), 1) < BAND - 2
    )
    mean = dot(onehot(member, f32), exw[...], precision=highest) * (1.0 / (GRID * GRID))
    top, low = halves(mean)
    stack = jnp.concatenate([top, low], axis=0)
    both = dot(stack, w[:, TAIL:LANES])
    reduced = both[0:8] + both[8:16]
    turned = pltpu.roll(swish(reduced), ex - sq, 1)
    lane = iota(turned.shape, 1)
    turned = jnp.where((lane >= ex) & (lane < dep), turned, 0.0)
    top, low = halves(turned)
    stack = jnp.concatenate([top, low], axis=0)
    both = dot(stack, w[:, TAIL:LANES], NT)
    excite = sigmoid(both[0:8] + both[8:16])
    exw[...] = by_band([excite[f:f + 1] for f in range(n_frames)])
    for r in range(bands):
        band = slice(r * BAND, (r + 1) * BAND)
        h[band, :] = (d[band, :] * exw[...]).astype(bf16)
    moves[-1].wait()
    block = dot(h[...], w[:, 0:width])
    mixed = (
        block.reshape(bands, BAND, width) * scale_band[None] + shift_band[None]
    ).reshape(rows, width)
    carry_out[0:rows, :] = mixed
    tiled = jnp.concatenate([learner[...]] * n_frames, axis=0)
    logits = dot(tiled, mixed, NT, highest)
    at = iota(logits.shape, 1) % BAND
    mine = (at % n_frames == iota(logits.shape, 0) // n_tokens) & (at < BAND - 2)
    attend = jnp.where(mine, sigmoid(logits), 0.0)
    carry_out[rows:rows + n_frames * n_tokens, 0:rows] = attend
    tokens = dot(attend, mixed, precision=highest) * (1.0 / (GRID * GRID))
    tokens = tokens.astype(bf16)
    for k in range(tokens_out.shape[0]):
        tokens_out[k] = tokens


def slots_onehot(dest, peers, capacity):
    count = dest.shape[1]
    named = iota((peers, count), 0) == dest
    before = onehot(iota((count, count), 0) < iota((count, count), 1))
    ahead = dot(onehot(named), before)
    place = jnp.sum(jnp.where(named, ahead, 0.0), axis=0, keepdims=True)
    slot = dest * capacity + place.astype(jnp.int32)
    return onehot(iota((peers * capacity, count), 0) == slot)


def scatter_kernel(peers, capacity, tokens, dest, after, out):
    del after
    out[...] = dot(slots_onehot(dest[...], peers, capacity), tokens[...]).astype(bf16)


def pick_kernel(peers, capacity, arrived, dest, out):
    chosen = dot(slots_onehot(dest[...], peers, capacity), arrived[...], TN)
    each = out.shape[1]
    for k in range(out.shape[0]):
        out[k] = chosen[k * each:(k + 1) * each].astype(bf16)


def backward_kernel(n_tokens, cells, carry, learner, grads, *outs):
    n_frames = 3
    *far, res = outs
    share = far[0].shape[1]
    rows = GRID * BAND
    mixed = carry[0:rows, :]
    held = carry[rows:rows + n_frames * n_tokens, 0:rows]
    scale = carry[rows + n_frames * n_tokens:, :]
    grad = grads[0].astype(f32)
    for k in range(1, grads.shape[0]):
        grad = grad + grads[k].astype(f32)
    inner = dot(grad, mixed, NT, highest)
    slope = inner * (1.0 / (GRID * GRID)) * held * (1.0 - held)
    both = jnp.concatenate([held * (1.0 / (GRID * GRID)), slope], axis=0)
    shape = (mixed.shape[0], n_frames * 128)
    row, lane = iota(shape, 0), iota(shape, 1)
    cell, frame = lane % 128, lane // 128
    spot = (row == cell // GRID * BAND + cell % GRID * n_frames + frame) & (cell < cells)
    both = dot(both, onehot(spot, f32), precision=highest)
    factors = jnp.concatenate([grad] + [learner[...]] * n_frames, axis=0)
    for f in range(n_frames):
        lanes = slice(f * 128, (f + 1) * 128)
        res[:, lanes] = dot(factors * scale[f:f + 1, :], both[:, lanes], TN, highest)
    me = lax.axis_index("mp")
    for k, out in enumerate(far):
        near = out.shape[0]
        for j in range(near):
            first = pl.multiple_of(lax.bitwise_xor(me, near * k + j) * share, 8)
            out[j] = res[pl.ds(first, share), :].astype(bf16)


def join_kernel(after, *refs):
    del after
    parts, outs = refs[:len(refs) // 2 + 1], refs[len(refs) // 2 + 1:]
    for j, out in enumerate(outs):
        for k, part in enumerate(parts):
            out[k] = part[j + 1]


def project_kernel(rows, weights, after, out):
    del after
    step = rows.shape[0] // 3
    for k in range(3):
        band = slice(k * step, (k + 1) * step)
        out[band, :] = dot(rows[band, :], weights[...]).astype(bf16)


def settle_kernel(*refs):
    *parts, out = refs
    n_frames = 3
    cells = out.shape[2]
    me = lax.axis_index("mp")
    near = parts[0].shape[0]
    far, joined = parts[:len(parts) - near + 1], parts[len(parts) - near + 1:]
    for k in range(len(far)):
        for j in range(near):
            block = far[k][0] if j == 0 else joined[j - 1][k]
            source = lax.bitwise_xor(me, near * k + j) * n_frames
            for f in range(n_frames):
                out[source + f] = block[:, f * 128:f * 128 + cells]


def per_device(
    frames,
    instr_ids,
    film_table,
    w_expand,
    w_depth,
    w_squeeze,
    w_excite,
    w_project,
    w_learner,
    token_dest,
    w_policy,
    policy_cot,
):
    count, cells, c_in = frames.shape
    width = w_project.shape[1]
    n_tokens = w_learner.shape[1]
    n_mp = lax.axis_size("mp")
    peers = lax.axis_size("seq")
    capacity = policy_cot.shape[0] // peers
    share = width // n_mp
    n_frames = count // n_mp
    c_se = w_squeeze.shape[1]
    rows = GRID * BAND
    hidden = n_mp * SHARD
    plan = lane_plan(width, c_in, c_se)
    sds = jax.ShapeDtypeStruct
    vmem = pl.BlockSpec(memory_space=pltpu.VMEM)
    dest = token_dest.T
    learner = w_learner.T

    raw = (w_expand.T, w_project, w_squeeze.T, w_excite, w_depth)
    mine = call(
        functools.partial(pack_kernel, plan),
        sds((SHARD, LANES), bf16),
        *raw,
        in_specs=[pl.BlockSpec(memory_space=pl.ANY)] * len(raw),
        scratch=[pltpu.VMEM(a.shape, a.dtype) for a in raw]
        + [pltpu.SemaphoreType.DMA((len(raw),))],
        vmem=60,
    )
    across = [(m, m ^ 1) for m in range(n_mp)]
    packed = lax.all_gather(mine, "mp", axis=0, tiled=True)
    grad_part = dot(policy_cot, w_policy, NT).astype(bf16)
    arrived = lax.all_to_all(
        grad_part.reshape(peers, capacity, width), "seq", split_axis=0, concat_axis=0, tiled=True
    )
    picked = call(
        functools.partial(pick_kernel, peers, capacity),
        sds((n_mp, n_frames * n_tokens, width), bf16),
        arrived.reshape(peers * capacity, width), dest,
        flops=3e8, moved=2e6,
    )
    grads = lax.all_to_all(picked, "mp", split_axis=0, concat_axis=0, tiled=True)

    own = lax.dynamic_slice_in_dim(frames, lax.axis_index("mp") * n_frames, n_frames, 0)
    own = own.transpose(1, 0, 2).reshape(GRID, GRID * n_frames, c_in)
    own = jnp.pad(own, ((0, 0), (0, BAND - GRID * n_frames), (0, 256 - c_in)))
    own = own.reshape(rows, 256)
    copies, carry = call(
        functools.partial(trunk_kernel, plan, n_tokens),
        (
            sds((n_mp, n_frames * n_tokens, width), bf16),
            sds((rows + n_frames * n_tokens + 8, width), f32),
        ),
        instr_ids, own, film_table, learner, packed, picked,
        in_specs=[pl.BlockSpec(memory_space=pltpu.SMEM)] + [pl.BlockSpec(memory_space=pl.ANY)] * 5,
        scratch=[
            pltpu.VMEM((hidden, LANES), bf16),
            pltpu.VMEM((rows, hidden), f32),
            pltpu.VMEM((rows, hidden), f32),
            pltpu.VMEM((rows, hidden), bf16),
            pltpu.VMEM((16, hidden), f32),
            pltpu.VMEM((BAND, hidden), f32),
            pltpu.VMEM((rows, 256), bf16),
            pltpu.VMEM((n_frames, 2, width), f32),
            pltpu.VMEM((n_tokens, width), f32),
            pltpu.SemaphoreType.DMA((4 + n_frames,)),
        ],
        flops=2e9, moved=3e7, vmem=58,
    )
    tokens = lax.all_to_all(copies, "mp", split_axis=0, concat_axis=0, tiled=True)
    near = 4
    blocks = sds((near, share, n_frames * 128), bf16)
    parts = call(
        functools.partial(backward_kernel, n_tokens, cells),
        (blocks,) * (n_mp // near),
        carry, learner, grads,
        scratch=[pltpu.VMEM((width, n_frames * 128), f32)],
        flops=1e9, moved=2e6,
    )

    def swap(value, far):
        return lax.ppermute(value, "mp", [(m, m ^ far) for m in range(n_mp)]) if far else value

    parts = [swap(part, near * k) for k, part in enumerate(parts)]
    outgoing = call(
        functools.partial(scatter_kernel, peers, capacity),
        sds((peers * capacity, width), bf16),
        tokens.reshape(count * n_tokens, width), dest, parts[1],
        in_specs=[vmem, vmem, pl.BlockSpec(memory_space=pl.ANY)],
        flops=3e8, moved=2e6,
    )
    joined = call(join_kernel, (blocks,) * (near - 1), outgoing, *parts,
                  in_specs=[pl.BlockSpec(memory_space=pl.ANY)] + [vmem] * len(parts))
    ready = joined[0]
    joined = [swap(part, j + 1) for j, part in enumerate(joined)]
    rows_in = lax.all_to_all(
        outgoing.reshape(peers, capacity, width), "seq", split_axis=0, concat_axis=0, tiled=True
    )
    feature_grad = call(settle_kernel, sds((count, share, cells), bf16), *parts, *joined)
    policy_in = call(
        project_kernel,
        sds((peers * capacity, w_policy.shape[1]), bf16),
        rows_in.reshape(peers * capacity, width), w_policy, ready,
        in_specs=[vmem, vmem, pl.BlockSpec(memory_space=pl.ANY)],
        flops=3e8, moved=2e6,
    )
    feature_grad = feature_grad.transpose(0, 2, 1)
    return (policy_in, feature_grad)


def solution(mesh):
    return jax.shard_map(
        per_device,
        mesh=mesh,
        in_specs=(
            P("seq", None, None),
            P("seq"),
            P(),
            P(None, "mp"),
            P(None, "mp"),
            P("mp", None),
            P(None, "mp"),
            P("mp", None),
            P(),
            P("seq", None),
            P(None, "mp"),
            P("seq", "mp"),
        ),
        out_specs=(P("seq", "mp"), P("seq", None, "mp")),
        check_vma=False,
    )
```
